512 devices in a mesh: dp: 16 (over x, y_lo, core), mp: 32 (over z, y_hi).
Axes of the slice: x: 4, y: 4 (y_hi: 2, y_lo: 2; y = y_hi * 2 + y_lo), z: 16, core: 2. Of those that a mesh axis runs over, the one named last changes fastest.
Arguments:
- tokens: bfloat16 [4096, 3072], P('dp'), may hold values from -6 to 6
- layer_norm_gain: float32 [3072], replicated, may hold values from 0.5 to 1.5
- w_qkv: bfloat16 [3072, 12288], P('dp', 'mp'), may hold values from -0.109375 to 0.109375
- q_gain: float32 [32, 128], P('mp'), may hold values from 0.5 to 1.5
- k_gain: float32 [32, 128], P('mp'), may hold values from 0.5 to 1.5
- ctx_grad: bfloat16 [4096, 4096], P('dp', 'mp'), may hold values from -12 to 12
Outputs:
- context: bfloat16 [4096, 4096], P('dp', 'mp')
- input_gradient_rows: bfloat16 [4096, 3072], P('dp', 'mp')
- layer_norm_gain_gradient: float32 [3072], P('mp')
- w_grad: bfloat16 [3072, 12288], P('dp', 'mp')
- q_gain_grad: float32 [32, 128], P('mp')
- k_gain_grad: float32 [32, 128], P('mp')
The draws below stay inside these ranges and needn't reach their ends.
All inputs are finite; a program needn't handle non-finite values.
Results may differ from the reference program's by a relative error of at most 0.025.
Values may be sent and summed in bfloat16 or wider, within the bound.
No kernel may reach another device: no remote copies, remote signals or barrier semaphores. Data moves between devices by JAX's collectives and lax.ppermute only.
A program may use at most 64 MiB of HBM per device.

```python
import jax
import jax.numpy as jnp
from jax import lax

D = 3072
HEADS = 32
HD = 128
PATCHES = 256
IMG_DEV = 1
IMAGES = 16
TOKENS = 4096
INNER = 4096
N_DP = 16
N_MP = 32


def levels(stream_key, dims, cuts, low, largest):
    level, own = 1.0, jax.random.fold_in(stream_key, 6)
    for axis_at, shards_of in cuts:
        steps = jnp.exp(jax.random.uniform(jax.random.fold_in(own, axis_at), (shards_of,), jnp.float32, low / len(cuts), largest / len(cuts)))
        level = level * jnp.repeat(steps, dims[axis_at] // shards_of).reshape([-1 if axis == axis_at else 1 for axis in range(len(dims))])
    return level


def scatter_about(rng, shape, width, reach, pieces=(), kind=jnp.bfloat16):
    gain = levels(rng, shape, pieces, -0.22, 0.18) if pieces else 1.0
    entries = jax.random.normal(rng, shape, jnp.float32) * width * gain
    return jnp.minimum(jnp.maximum(entries, -reach), reach).astype(kind)


def setup_inputs(seed: int = 0) -> dict:
    key_of = jax.random.split(jax.random.key(seed), 7)
    tokens = scatter_about(key_of[0], (TOKENS, D), 1.0, 6.0, ((0, 16),))
    layer_norm_gain = jnp.clip(1.0 + 0.1 * jax.random.normal(key_of[1], (D,), jnp.float32), 0.5, 1.5)
    w_qkv = scatter_about(key_of[2], (D, 3 * INNER), D ** -0.5, 0.109375, ((0, 16), (1, 32)))
    q_gain = jnp.clip(1.0 + 0.1 * jax.random.normal(key_of[3], (HEADS, HD), jnp.float32), 0.5, 1.5)
    k_gain = jnp.clip(1.0 + 0.1 * jax.random.normal(key_of[4], (HEADS, HD), jnp.float32), 0.5, 1.5)
    ctx_grad = scatter_about(key_of[5], (TOKENS, INNER), 2.0, 12.0, ((0, 16), (1, 32)))
    return {"tokens": tokens, "layer_norm_gain": layer_norm_gain, "w_qkv": w_qkv, "q_gain": q_gain, "k_gain": k_gain, "ctx_grad": ctx_grad}


def head_norm(raw):
    centered_input = raw - lax.optimization_barrier(jnp.mean(raw, axis=-1, keepdims=True))
    inverse_deviation = lax.rsqrt(lax.optimization_barrier(jnp.mean(centered_input * centered_input, axis=-1, keepdims=True)) + 1e-06)
    return (centered_input * inverse_deviation, inverse_deviation)

def norm_backward_pass(grad_hat, normal, inverse_deviation):
    first = lax.optimization_barrier(jnp.mean(grad_hat, axis=-1, keepdims=True))
    second = lax.optimization_barrier(jnp.mean(grad_hat * normal, axis=-1, keepdims=True))
    return (grad_hat - first - normal * second) * inverse_deviation

def attend(query_raw, key_raw, value_raw, grad, q_gain, k_gain):
    head_size = query_raw.shape[-1]
    scale = head_size ** (-0.5)
    qhat, q_inv = head_norm(query_raw)
    khat, k_inv = head_norm(key_raw)
    q_norm = (qhat * q_gain).astype(jnp.bfloat16)
    k_norm = (khat * k_gain).astype(jnp.bfloat16)
    value = value_raw.astype(jnp.bfloat16)
    scores = jnp.einsum('...qhd,...khd->...hqk', q_norm.astype(jnp.float32), k_norm.astype(jnp.float32)) * scale
    expo = jnp.exp(scores)
    probs = expo / lax.optimization_barrier(jnp.sum(expo, axis=-1, keepdims=True))
    probs_b = probs.astype(jnp.bfloat16)
    context = jnp.einsum('...hqk,...khd->...qhd', probs_b.astype(jnp.float32), value.astype(jnp.float32)).astype(jnp.bfloat16)
    grad_f = grad.astype(jnp.float32)
    dprob = jnp.einsum('...qhd,...khd->...hqk', grad_f, value.astype(jnp.float32))
    dvalue = jnp.einsum('...hqk,...qhd->...khd', probs_b.astype(jnp.float32), grad_f).astype(jnp.bfloat16)
    dscore = (probs * (dprob - lax.optimization_barrier(jnp.sum(probs * dprob, axis=-1, keepdims=True))) * scale).astype(jnp.bfloat16)
    dscore_f = dscore.astype(jnp.float32)
    dqn = jnp.einsum('...hqk,...khd->...qhd', dscore_f, k_norm.astype(jnp.float32))
    dkn = jnp.einsum('...hqk,...qhd->...khd', dscore_f, q_norm.astype(jnp.float32))
    lead = tuple(range(dqn.ndim - 2))
    q_part = lax.optimization_barrier(jnp.sum(dqn * qhat, axis=lead))
    k_part = lax.optimization_barrier(jnp.sum(dkn * khat, axis=lead))
    dquery = norm_backward_pass(dqn * q_gain, qhat, q_inv).astype(jnp.bfloat16)
    dkey = norm_backward_pass(dkn * k_gain, khat, k_inv).astype(jnp.bfloat16)
    return (context, dquery, dkey, dvalue, q_part, k_part)

def reference(tokens, layer_norm_gain, w_qkv, q_gain, k_gain, ctx_grad):
    x_float = tokens.astype(jnp.float32)
    centered_input = x_float - lax.optimization_barrier(jnp.mean(x_float, axis=-1, keepdims=True))
    inverse_deviation = lax.rsqrt(lax.optimization_barrier(jnp.mean(centered_input * centered_input, axis=-1, keepdims=True)) + 1e-06)
    standardized_input = centered_input * inverse_deviation
    normed_input = (standardized_input * layer_norm_gain).astype(jnp.bfloat16)
    qkv = jnp.dot(normed_input, w_qkv, preferred_element_type=jnp.float32)
    qkv = qkv.reshape(IMAGES, PATCHES, HEADS, 3, HD)
    grads = ctx_grad.reshape(IMAGES, PATCHES, HEADS, HD)

    def one_image(item):
        return attend(item[0], item[1], item[2], item[3], q_gain, k_gain)
    context, dquery, dkey, dvalue, q_parts, k_parts = lax.map(one_image, (qkv[:, :, :, 0], qkv[:, :, :, 1], qkv[:, :, :, 2], grads))
    context = context.reshape(TOKENS, INNER)
    dqkv = jnp.stack([dquery, dkey, dvalue], axis=3).reshape(TOKENS, 3 * INNER)
    q_gain_grad = lax.optimization_barrier(jnp.sum(q_parts, axis=0))
    k_gain_grad = lax.optimization_barrier(jnp.sum(k_parts, axis=0))
    rows = IMG_DEV * PATCHES

    def add_group(total, group):
        start = group * rows
        part_x = lax.dynamic_slice_in_dim(normed_input, start, rows, 0)
        part_g = lax.dynamic_slice_in_dim(dqkv, start, rows, 0)
        term = lax.dot_general(part_x, part_g, (((0,), (0,)), ((), ())), preferred_element_type=jnp.float32)
        term = lax.optimization_barrier(term.astype(jnp.bfloat16)).astype(jnp.float32)
        return (total + term, None)
    w_total, _ = lax.scan(add_group, jnp.zeros((D, 3 * INNER), jnp.float32), jnp.arange(N_DP, dtype=jnp.int32))
    w_grad = w_total.astype(jnp.bfloat16)
    feature_width = 3 * HD * HEADS // N_MP

    def add_heads(total, group):
        start = group * feature_width
        part_g = lax.dynamic_slice_in_dim(dqkv, start, feature_width, 1)
        part_w = lax.dynamic_slice_in_dim(w_qkv, start, feature_width, 1)
        term = lax.dot_general(part_g, part_w, (((1,), (1,)), ((), ())), preferred_element_type=jnp.float32)
        term = lax.optimization_barrier(term.astype(jnp.bfloat16)).astype(jnp.float32)
        return (total + term, None)
    normed_gradient, _ = lax.scan(add_heads, jnp.zeros((TOKENS, D), jnp.float32), jnp.arange(N_MP, dtype=jnp.int32))
    layer_norm_gain_gradient = lax.optimization_barrier(jnp.sum(normed_gradient * standardized_input, axis=0))
    input_gradient_rows = norm_backward_pass(normed_gradient * layer_norm_gain, standardized_input, inverse_deviation).astype(jnp.bfloat16)
    return (context, input_gradient_rows, layer_norm_gain_gradient, w_grad, q_gain_grad, k_gain_grad)
```

```python
import jax
import jax.numpy as jnp
from jax import lax
from jax.sharding import PartitionSpec as P

BF = jnp.bfloat16
F32 = jnp.float32
PATCHES = 256
DP, MP = "dp", "mp"
NX, NYL, NC = 4, 2, 2
NZ, NYH = 16, 2

CORE_SWAP = [(i, i ^ 1) for i in range(NX * NYL * NC)]
SAME_CORE = [[2 * i + c for i in range(NX * NYL)] for c in range(NC)]
YHI_SWAP = [(j, j ^ 1) for j in range(NZ * NYH)]
SAME_YHI = [[2 * z + y for z in range(NZ)] for y in range(NYH)]


def head_norm(raw):
    centered = raw - jnp.mean(raw, axis=-1, keepdims=True)
    inverse = lax.rsqrt(jnp.mean(centered * centered, axis=-1, keepdims=True) + 1e-06)
    return centered * inverse, inverse


def norm_backward_pass(grad_hat, normal, inverse):
    first = jnp.mean(grad_hat, axis=-1, keepdims=True)
    second = jnp.mean(grad_hat * normal, axis=-1, keepdims=True)
    return (grad_hat - first - normal * second) * inverse


def dot(a, b, ca, cb):
    return lax.dot_general(a, b, (((ca,), (cb,)), ((), ())), preferred_element_type=F32)


def attend(raw, grad, q_gain, k_gain):
    hd = q_gain.shape[-1]
    scale = hd ** (-0.5)
    qhat, q_inv = head_norm(raw[:, :hd])
    khat, k_inv = head_norm(raw[:, hd : 2 * hd])
    value = raw[:, 2 * hd :].astype(BF)
    q_norm = (qhat * q_gain).astype(BF)
    k_norm = (khat * k_gain).astype(BF)
    expo = jnp.exp(dot(q_norm, k_norm, 1, 1) * scale)
    probs = expo / jnp.sum(expo, axis=-1, keepdims=True)
    probs_b = probs.astype(BF)
    context = dot(probs_b, value, 1, 0).astype(BF)
    dprob = dot(grad, value, 1, 1)
    dvalue = dot(probs_b, grad, 0, 0).astype(BF)
    dscore = (probs * (dprob - jnp.sum(probs * dprob, axis=-1, keepdims=True)) * scale).astype(BF)
    dqn = dot(dscore, k_norm, 1, 0)
    dkn = dot(dscore, q_norm, 0, 0)
    q_part = jnp.sum(dqn * qhat, axis=0, keepdims=True)
    k_part = jnp.sum(dkn * khat, axis=0, keepdims=True)
    dquery = norm_backward_pass(dqn * q_gain, qhat, q_inv).astype(BF)
    dkey = norm_backward_pass(dkn * k_gain, khat, k_inv).astype(BF)
    return context, jnp.concatenate([dquery, dkey, dvalue], axis=1), q_part, k_part


def hi_lo(value):
    hi = value.astype(BF)
    lo = (value - hi.astype(F32)).astype(BF)
    return hi, lo


def per_device(tokens, layer_norm_gain, w_qkv, q_gain, k_gain, ctx_grad):
    rows, width = tokens.shape
    w_rows, columns = w_qkv.shape
    share = width // (NZ * NYH)
    core = lax.axis_index(DP) % 2
    y_hi = lax.axis_index(MP) % 2
    mp = lax.axis_index(MP)

    with jax.named_scope("gather_w"):
        copies = jnp.broadcast_to(w_qkv[None], (NX * NYL, w_rows, columns))
        own = lax.all_to_all(copies, DP, 0, 0, axis_index_groups=SAME_CORE, tiled=True)
        other = lax.ppermute(own, DP, CORE_SWAP)
        full = jnp.stack(
            [jnp.where(core == 0, own, other), jnp.where(core == 0, other, own)], axis=1
        ).reshape(width, columns)

    with jax.named_scope("input_norm"):
        x_float = tokens.astype(F32)
        centered = x_float - jnp.mean(x_float, axis=-1, keepdims=True)
        inverse = lax.rsqrt(jnp.mean(centered * centered, axis=-1, keepdims=True) + 1e-06)
        xhat = centered * inverse
        normed = (xhat * layer_norm_gain).astype(BF)

    with jax.named_scope("attention"):
        qkv = dot(normed, full, 1, 0)
        context, dqkv, q_part, k_part = attend(qkv, ctx_grad, q_gain, k_gain)

    with jax.named_scope("input_gradient_partial"):
        dqkv_f = dqkv.astype(F32)
        weighted = jnp.sum(full.astype(F32) * layer_norm_gain[:, None], axis=0)
        s1 = jnp.sum(dqkv_f * weighted[None, :], axis=1)
        s2 = jnp.sum(dqkv_f * qkv, axis=1)
        by_y = full.reshape(NZ, NYH, share, columns)
        w_keep = jnp.where(y_hi == 0, by_y[:, 0], by_y[:, 1]).reshape(-1, columns)
        w_send = jnp.where(y_hi == 0, by_y[:, 1], by_y[:, 0]).reshape(-1, columns)
        part_send = dot(w_send, dqkv, 1, 1).astype(BF)
        part_keep = dot(w_keep, dqkv, 1, 1)
        h1, l1 = hi_lo(s1)
        h2, l2 = hi_lo(s2)
        sums = jnp.concatenate(
            [jnp.stack([h1, l1, h2, l2]), jnp.zeros((12, rows), BF)], axis=0
        )
        got = lax.ppermute(part_send, MP, YHI_SWAP).astype(F32)
        got_sums = lax.ppermute(sums, MP, YHI_SWAP).astype(F32)
        t1 = s1 + got_sums[0] + got_sums[1]
        t2 = s2 + got_sums[2] + got_sums[3]
        h1, l1 = hi_lo(t1)
        h2, l2 = hi_lo(t2)
        sums = jnp.concatenate(
            [jnp.stack([h1, l1, h2, l2]), jnp.zeros((12, rows), BF)], axis=0
        )
        pair = (part_keep + got).astype(BF).reshape(NZ, share, rows)
        pair = jnp.concatenate([pair, jnp.broadcast_to(sums[None], (NZ, 16, rows))], axis=1)

    with jax.named_scope("w_grad"):
        term = dot(normed, dqkv, 0, 0).astype(BF).reshape(NX * NYL, NC, w_rows, columns)
        term_keep = jnp.where(core == 0, term[:, 0], term[:, 1])
        term_send = jnp.where(core == 0, term[:, 1], term[:, 0])
        term_got = lax.ppermute(term_send, DP, CORE_SWAP)
        chip = (term_keep.astype(F32) + term_got.astype(F32)).astype(BF)
        w_grad = lax.psum_scatter(
            chip.reshape(-1, columns), DP, scatter_dimension=0, tiled=True,
            axis_index_groups=SAME_CORE,
        )

    with jax.named_scope("sum_over_z"):
        parts = lax.all_to_all(pair, MP, 0, 0, axis_index_groups=SAME_YHI, tiled=True)
        total = jnp.sum(parts.astype(F32), axis=0)
        dnormed = total[:share].T
        plain = (total[share] + total[share + 1])[:, None]
        cross = (total[share + 2] + total[share + 3])[:, None]

    with jax.named_scope("input_gradient"):
        start = mp * share
        xhat_share = lax.dynamic_slice_in_dim(xhat, start, share, 1)
        gain_share = lax.dynamic_slice_in_dim(layer_norm_gain, start, share, 0)
        input_gradient_rows = (
            (dnormed * gain_share - plain / width - xhat_share * (cross / width)) * inverse
        ).astype(BF)
        gain_portion = jnp.sum(dnormed * xhat_share, axis=0)

    with jax.named_scope("gain_gradients"):
        small = jnp.concatenate(
            [
                jnp.pad(gain_portion, (0, 128 - share))[None],
                q_part,
                k_part,
                jnp.zeros((5, 128), F32),
            ],
            axis=0,
        )
        copies = jnp.broadcast_to(small[None], (NX * NYL * NC, 8, 128))
        summed = jnp.sum(lax.all_to_all(copies, DP, 0, 0, tiled=True), axis=0)
    return (
        context,
        input_gradient_rows,
        summed[0, :share],
        w_grad,
        summed[1:2],
        summed[2:3],
    )


def solution(mesh):
    placed = (P("dp", None), P(), P("dp", "mp"), P("mp", None), P("mp", None), P("dp", "mp"))
    return jax.shard_map(
        per_device,
        mesh=mesh,
        in_specs=placed,
        out_specs=(
            P("dp", "mp"),
            P("dp", "mp"),
            P("mp"),
            P("dp", "mp"),
            P("mp", None),
            P("mp", None),
        ),
        check_vma=False,
    )
```

```python
import jax
import jax.numpy as jnp
from jax import lax
from jax.sharding import PartitionSpec as P

BF = jnp.bfloat16
F32 = jnp.float32
PATCHES = 256
DP, MP = "dp", "mp"
NX, NYL, NC = 4, 2, 2
NZ, NYH = 16, 2

CORE_SWAP = [(i, i ^ 1) for i in range(NX * NYL * NC)]
SAME_CORE = [[2 * i + c for i in range(NX * NYL)] for c in range(NC)]
YHI_SWAP = [(j, j ^ 1) for j in range(NZ * NYH)]
Z_PAIR = [(2 * z + y, 2 * (z ^ 1) + y) for z in range(NZ) for y in range(NYH)]
Z_BETWEEN = [
    (2 * z + y, 2 * ((z + 1 if z % 2 else z - 1) % NZ) + y)
    for z in range(NZ)
    for y in range(NYH)
]
Z_PARITY = [[2 * (2 * k + p) + y for k in range(NZ // 2)] for p in range(2) for y in range(NYH)]


def head_norm(raw):
    centered = raw - jnp.mean(raw, axis=-1, keepdims=True)
    inverse = lax.rsqrt(jnp.mean(centered * centered, axis=-1, keepdims=True) + 1e-06)
    return centered * inverse, inverse


def norm_backward_pass(grad_hat, normal, inverse):
    first = jnp.mean(grad_hat, axis=-1, keepdims=True)
    second = jnp.mean(grad_hat * normal, axis=-1, keepdims=True)
    return (grad_hat - first - normal * second) * inverse


def dot(a, b, ca, cb):
    return lax.dot_general(a, b, (((ca,), (cb,)), ((), ())), preferred_element_type=F32)


def attend(raw, grad, q_gain, k_gain):
    hd = q_gain.shape[-1]
    scale = hd ** (-0.5)
    qhat, q_inv = head_norm(raw[:, :hd])
    khat, k_inv = head_norm(raw[:, hd : 2 * hd])
    value = raw[:, 2 * hd :].astype(BF)
    q_norm = (qhat * q_gain).astype(BF)
    k_norm = (khat * k_gain).astype(BF)
    expo = jnp.exp(dot(q_norm, k_norm, 1, 1) * scale)
    probs = expo / jnp.sum(expo, axis=-1, keepdims=True)
    probs_b = probs.astype(BF)
    context = dot(probs_b, value, 1, 0).astype(BF)
    dprob = dot(grad, value, 1, 1)
    dvalue = dot(probs_b, grad, 0, 0).astype(BF)
    dscore = (probs * (dprob - jnp.sum(probs * dprob, axis=-1, keepdims=True)) * scale).astype(BF)
    dqn = dot(dscore, k_norm, 1, 0)
    dkn = dot(dscore, q_norm, 0, 0)
    q_part = jnp.sum(dqn * qhat, axis=0, keepdims=True)
    k_part = jnp.sum(dkn * khat, axis=0, keepdims=True)
    dquery = norm_backward_pass(dqn * q_gain, qhat, q_inv).astype(BF)
    dkey = norm_backward_pass(dkn * k_gain, khat, k_inv).astype(BF)
    return context, jnp.concatenate([dquery, dkey, dvalue], axis=1), q_part, k_part


def hi_lo(value):
    hi = value.astype(BF)
    lo = (value - hi.astype(F32)).astype(BF)
    return hi, lo


def pack(sums):
    hi, lo = hi_lo(sums)
    return jnp.where(lax.broadcasted_iota(jnp.int32, sums.shape, 0) < 2, hi, lo)


def unpack(sums, got):
    got = got.astype(F32)
    both = got[0:2] + got[2:4]
    return sums + jnp.concatenate([both] * 8, axis=0)


def per_device(tokens, layer_norm_gain, w_qkv, q_gain, k_gain, ctx_grad):
    rows, width = tokens.shape
    w_rows, columns = w_qkv.shape
    share = width // (NZ * NYH)
    core = lax.axis_index(DP) % 2
    y_hi = lax.axis_index(MP) % 2
    mp = lax.axis_index(MP)
    parity = (mp // 2) % 2

    with jax.named_scope("gather_w"):
        copies = jnp.broadcast_to(w_qkv[None], (NX * NYL, w_rows, columns))
        own = lax.all_to_all(copies, DP, 0, 0, axis_index_groups=SAME_CORE, tiled=True)
        other = lax.ppermute(own, DP, CORE_SWAP)
        full = jnp.stack(
            [jnp.where(core == 0, own, other), jnp.where(core == 0, other, own)], axis=1
        ).reshape(width, columns)

    with jax.named_scope("input_norm"):
        x_float = tokens.astype(F32)
        centered = x_float - jnp.mean(x_float, axis=-1, keepdims=True)
        inverse = lax.rsqrt(jnp.mean(centered * centered, axis=-1, keepdims=True) + 1e-06)
        xhat = centered * inverse
        normed = (xhat * layer_norm_gain).astype(BF)

    with jax.named_scope("attention"):
        qkv = dot(normed, full, 1, 0)
        context, dqkv, q_part, k_part = attend(qkv, ctx_grad, q_gain, k_gain)

    with jax.named_scope("patch_sums"):
        weighted = jnp.sum(full.astype(F32) * layer_norm_gain[:, None], axis=0, keepdims=True)
        row = lax.broadcasted_iota(jnp.int32, (16, columns), 0)
        is_first = ((row == 0) | (row == 2)).astype(F32)
        is_second = ((row == 1) | (row == 3)).astype(BF)
        w_hi, w_lo = hi_lo(is_first * weighted)
        p_hi, p_lo = hi_lo(dqkv.astype(F32) * qkv)
        sums = (dot(w_hi, dqkv, 1, 1) + dot(w_lo, dqkv, 1, 1)) + (
            dot(is_second, p_hi, 1, 1) + dot(is_second, p_lo, 1, 1)
        )

    with jax.named_scope("input_gradient_partial"):
        half = share // 2
        lane = rows // 2
        by = full.reshape(NZ // 2, 2, NYH, share, columns)
        pick = lambda which, at, dim: jnp.where(
            which == 0, lax.index_in_dim(at, 0, dim, False), lax.index_in_dim(at, 1, dim, False)
        ).reshape(-1, columns)
        w_a, w_b = by[:, :, :, :half], by[:, :, :, half:]
        send_a = dot(pick(1 - y_hi, w_a, 2), dqkv, 1, 1).astype(BF)
        send_b = dot(pick(1 - parity, w_b, 1), dqkv, 1, 1).astype(BF)
        send_a = jnp.concatenate([send_a, pack(sums)], axis=0)
        got_a = lax.ppermute(send_a, MP, YHI_SWAP)
        got_b0 = lax.ppermute(send_b[:, :lane], MP, Z_PAIR)
        got_b1 = lax.ppermute(send_b[:, lane:], MP, Z_BETWEEN)
        keep_a = dot(pick(y_hi, w_a, 2), dqkv, 1, 1)
        keep_b = dot(pick(parity, w_b, 1), dqkv, 1, 1)

    with jax.named_scope("w_grad"):
        term = dot(normed, dqkv, 0, 0).astype(BF).reshape(NX * NYL, NC, w_rows, columns)
        term_keep = jnp.where(core == 0, term[:, 0], term[:, 1])
        term_send = jnp.where(core == 0, term[:, 1], term[:, 0])
        term_got = lax.ppermute(term_send, DP, CORE_SWAP)
        chip = (term_keep.astype(F32) + term_got.astype(F32)).astype(BF)
        chip, got_a, got_b0, got_b1 = lax.optimization_barrier((chip, got_a, got_b0, got_b1))
        w_grad = lax.psum_scatter(
            chip.reshape(-1, columns), DP, scatter_dimension=0, tiled=True,
            axis_index_groups=SAME_CORE,
        )

    with jax.named_scope("sum_over_pairs"):
        many = (NZ // 2) * 2 * half
        a = (keep_a + got_a[:many].astype(F32)).reshape(NZ // 2, 2, half, rows)
        sums = unpack(sums, got_a[many:])
        b = (keep_b + jnp.concatenate([got_b0, got_b1], axis=1).astype(F32)).reshape(
            NZ // 2, NYH, half, rows
        )
        flat = (NZ // 2 * half, rows)
        a_send = jnp.where(parity == 0, a[:, 1], a[:, 0]).astype(BF).reshape(flat)
        b_send = jnp.where(y_hi == 0, b[:, 1], b[:, 0]).astype(BF).reshape(flat)
        a_keep = jnp.where(parity == 0, a[:, 0], a[:, 1])
        b_keep = jnp.where(y_hi == 0, b[:, 0], b[:, 1])
        packed = pack(sums)
        packed = jnp.concatenate([packed[:, :lane], packed[:, lane:]], axis=0)
        got_b = lax.ppermute(b_send, MP, YHI_SWAP)
        got_a0 = lax.ppermute(
            jnp.concatenate([a_send[:, :lane], packed], axis=0), MP, Z_PAIR
        )
        got_a1 = lax.ppermute(a_send[:, lane:], MP, Z_BETWEEN)
        many = NZ // 2 * half
        got_sums = jnp.concatenate([got_a0[many : many + 16], got_a0[many + 16 :]], axis=1)
        sums = unpack(sums, got_sums)
        got_a = jnp.concatenate([got_a0[:many], got_a1], axis=1)
        a = (a_keep + got_a.astype(F32).reshape(a_keep.shape)).astype(BF)
        b = (b_keep + got_b.astype(F32).reshape(b_keep.shape)).astype(BF)

    with jax.named_scope("sum_over_z"):
        riding = jnp.broadcast_to(pack(sums)[None], (NZ // 2, 16, rows))
        parts = lax.all_to_all(
            jnp.concatenate([a, b, riding], axis=1), MP, 0, 0,
            axis_index_groups=Z_PARITY, tiled=True,
        )
        total = jnp.sum(parts.astype(F32), axis=0)
        dnormed = total[:share]
        plain = total[share : share + 1] + total[share + 2 : share + 3]
        cross = total[share + 1 : share + 2] + total[share + 3 : share + 4]

    with jax.named_scope("input_gradient"):
        start = mp * share
        xhat_share = lax.dynamic_slice_in_dim(xhat, start, share, 1).T
        gain_share = lax.dynamic_slice_in_dim(layer_norm_gain, start, share, 0)
        input_gradient_rows = (
            (dnormed * gain_share[:, None] - plain / width - xhat_share * (cross / width))
            * inverse.T
        ).T.astype(BF)
        gain_portion = jnp.sum(dnormed * xhat_share, axis=1)

    with jax.named_scope("gain_gradients"):
        small = jnp.concatenate(
            [
                jnp.pad(gain_portion, (0, 128 - share))[None],
                q_part,
                k_part,
                jnp.zeros((5, 128), F32),
            ],
            axis=0,
        )
        copies = jnp.broadcast_to(small[None], (NX * NYL * NC, 8, 128))
        summed = jnp.sum(lax.all_to_all(copies, DP, 0, 0, tiled=True), axis=0)
    return (
        context,
        input_gradient_rows,
        summed[0, :share],
        w_grad,
        summed[1:2],
        summed[2:3],
    )


def solution(mesh):
    placed = (P("dp", None), P(), P("dp", "mp"), P("mp", None), P("mp", None), P("dp", "mp"))
    return jax.shard_map(
        per_device,
        mesh=mesh,
        in_specs=placed,
        out_specs=(
            P("dp", "mp"),
            P("dp", "mp"),
            P("mp"),
            P("dp", "mp"),
            P("mp", None),
            P("mp", None),
        ),
        check_vma=False,
    )
```

```python
import jax
import jax.numpy as jnp
from jax import lax
from jax.sharding import PartitionSpec as P

BF = jnp.bfloat16
F32 = jnp.float32
PATCHES = 256
DP, MP = "dp", "mp"
NX, NYL, NC = 4, 2, 2
NZ, NYH = 16, 2

CORE_SWAP = [(i, i ^ 1) for i in range(NX * NYL * NC)]
SAME_CORE = [[2 * i + c for i in range(NX * NYL)] for c in range(NC)]
YLO_SWAP = [(i, i ^ 2) for i in range(NX * NYL * NC)]
X_STEPS = [
    [(i, (i + step * NYL * NC) % (NX * NYL * NC)) for i in range(NX * NYL * NC)]
    for step in range(1, NX)
]
YHI_SWAP = [(j, j ^ 1) for j in range(NZ * NYH)]
SAME_YHI = [[2 * z + y for z in range(NZ)] for y in range(NYH)]


def head_norm(raw):
    centered = raw - jnp.mean(raw, axis=-1, keepdims=True)
    inverse = lax.rsqrt(jnp.mean(centered * centered, axis=-1, keepdims=True) + 1e-06)
    return centered * inverse, inverse


def norm_backward_pass(grad_hat, normal, inverse):
    first = jnp.mean(grad_hat, axis=-1, keepdims=True)
    second = jnp.mean(grad_hat * normal, axis=-1, keepdims=True)
    return (grad_hat - first - normal * second) * inverse


def dot(a, b, ca, cb):
    return lax.dot_general(a, b, (((ca,), (cb,)), ((), ())), preferred_element_type=F32)


def attend(raw, grad, q_gain, k_gain):
    hd = q_gain.shape[-1]
    scale = hd ** (-0.5)
    qhat, q_inv = head_norm(raw[:, :hd])
    khat, k_inv = head_norm(raw[:, hd : 2 * hd])
    value = raw[:, 2 * hd :].astype(BF)
    q_norm = (qhat * q_gain).astype(BF)
    k_norm = (khat * k_gain).astype(BF)
    expo = jnp.exp(dot(q_norm, k_norm, 1, 1) * scale)
    probs = expo / jnp.sum(expo, axis=-1, keepdims=True)
    probs_b = probs.astype(BF)
    context = dot(probs_b, value, 1, 0).astype(BF)
    dprob = dot(grad, value, 1, 1)
    dvalue = dot(probs_b, grad, 0, 0).astype(BF)
    dscore = (probs * (dprob - jnp.sum(probs * dprob, axis=-1, keepdims=True)) * scale).astype(BF)
    dqn = dot(dscore, k_norm, 1, 0)
    dkn = dot(dscore, q_norm, 0, 0)
    q_part = jnp.sum(dqn * qhat, axis=0, keepdims=True)
    k_part = jnp.sum(dkn * khat, axis=0, keepdims=True)
    dquery = norm_backward_pass(dqn * q_gain, qhat, q_inv).astype(BF)
    dkey = norm_backward_pass(dkn * k_gain, khat, k_inv).astype(BF)
    return context, jnp.concatenate([dquery, dkey, dvalue], axis=1), q_part, k_part


def hi_lo(value):
    hi = value.astype(BF)
    lo = (value - hi.astype(F32)).astype(BF)
    return hi, lo


def pack(sums):
    hi, lo = hi_lo(sums)
    row = lax.broadcasted_iota(jnp.int32, sums.shape, 0)
    rows = jnp.where(row % 4 < 2, hi, lo)
    return jnp.concatenate([rows, jnp.zeros_like(rows)], axis=0)


def unpack(got):
    got = got.astype(F32)
    first, second = got[0:2] + got[2:4], got[4:6] + got[6:8]
    return jnp.concatenate([first, first, second, second], axis=0)


def after(value, other):
    first = other.reshape(-1, other.shape[-1])[:1, :128].astype(F32)
    zero = jnp.minimum(jnp.abs(first), 0.0)
    return value + jnp.concatenate([zero] * (value.shape[-1] // 128), axis=1)


def per_device(tokens, layer_norm_gain, w_qkv, q_gain, k_gain, ctx_grad):
    rows, width = tokens.shape
    w_rows, columns = w_qkv.shape
    share = width // (NZ * NYH)
    core = lax.axis_index(DP) % 2
    y_lo = (lax.axis_index(DP) // NC) % NYL
    x_at = lax.axis_index(DP) // (NYL * NC)
    y_hi = lax.axis_index(MP) % 2
    mp = lax.axis_index(MP)
    lane = rows // 2

    with jax.named_scope("gather_w"):
        copies = jnp.broadcast_to(w_qkv[None], (NX * NYL, w_rows, columns))
        own = lax.all_to_all(copies, DP, 0, 0, axis_index_groups=SAME_CORE, tiled=True)
        other = lax.ppermute(own, DP, CORE_SWAP)
        full = jnp.stack(
            [jnp.where(core == 0, own, other), jnp.where(core == 0, other, own)], axis=1
        ).reshape(width, columns)

    with jax.named_scope("input_norm"):
        x_float = tokens.astype(F32)
        centered = x_float - jnp.mean(x_float, axis=-1, keepdims=True)
        inverse = lax.rsqrt(jnp.mean(centered * centered, axis=-1, keepdims=True) + 1e-06)
        xhat = centered * inverse
        normed = (xhat * layer_norm_gain).astype(BF)

    with jax.named_scope("attention"):
        qkv = dot(normed, full, 1, 0)
        context, dqkv, q_part, k_part = attend(qkv, ctx_grad, q_gain, k_gain)

    with jax.named_scope("patch_sums"):
        weighted = jnp.sum(full.astype(F32) * layer_norm_gain[:, None], axis=0, keepdims=True)
        row = lax.broadcasted_iota(jnp.int32, (8, columns), 0)
        w_hi, w_lo = hi_lo(jnp.where(row % 2 == 0, weighted, 0.0))
        ones = (row % 2 == 1).astype(BF)
        p_hi, p_lo = hi_lo(dqkv.astype(F32) * qkv)
        sums = (dot(w_hi, dqkv, 1, 1) + dot(w_lo, dqkv, 1, 1)) + (
            dot(ones, p_hi, 1, 1) + dot(ones, p_lo, 1, 1)
        )
        sums = jnp.concatenate([sums[:4, :lane], sums[:4, lane:]], axis=0)

    with jax.named_scope("input_gradient_partial"):
        by_y = full.reshape(NZ, NYH, share, columns)
        w_keep = jnp.where(y_hi == 0, by_y[:, 0], by_y[:, 1]).reshape(-1, columns)
        w_send = jnp.where(y_hi == 0, by_y[:, 1], by_y[:, 0]).reshape(-1, columns)
        send_a = dot(w_send, dqkv[:lane], 1, 1).astype(BF)
        got_a = lax.ppermute(send_a, MP, YHI_SWAP)

    with jax.named_scope("w_grad"):
        term = after(dot(normed, dqkv, 0, 0), send_a)
        term = term.astype(BF).reshape(NX * NYL, NC, w_rows, columns)
        term_keep = jnp.where(core == 0, term[:, 0], term[:, 1])
        term_send = jnp.where(core == 0, term[:, 1], term[:, 0])
        term_got = lax.ppermute(term_send, DP, CORE_SWAP)
        chip = (term_keep.astype(F32) + term_got.astype(F32)).astype(BF)

    with jax.named_scope("sum_over_y"):
        pair_a = dot(w_keep, dqkv[:lane], 1, 1) + got_a.astype(F32)
        pair_a = after(pair_a, chip).astype(BF).reshape(NZ, share, lane)
        send_b = after(dot(w_send, dqkv[lane:], 1, 1), pair_a)
        send_b = jnp.concatenate([send_b.astype(BF), pack(sums)], axis=0)
        got_b = lax.ppermute(send_b, MP, YHI_SWAP)

    with jax.named_scope("sum_over_y_second"):
        many = NZ * share
        pair_b = dot(w_keep, dqkv[lane:], 1, 1) + got_b[:many].astype(F32)
        pair_b = pair_b.astype(BF)
        sums = sums + unpack(got_b[many:])
        riding = jnp.broadcast_to(pack(sums)[None], (NZ, 16, lane))
        pair_b = jnp.concatenate([pair_b.reshape(NZ, share, lane), riding], axis=1)

    with jax.named_scope("w_grad_chips"):
        ready = after(chip.astype(F32), send_b).astype(BF).reshape(NX, NYL, w_rows, columns)
        x_term = lax.dynamic_index_in_dim(ready, x_at, 0, False).astype(F32)
        for step, pairs in enumerate(X_STEPS, 1):
            leaves = lax.dynamic_index_in_dim(ready, (x_at + step) % NX, 0, False)
            x_term = x_term + lax.ppermute(leaves, DP, pairs).astype(F32)
        x_term = after(x_term, pair_b)
        leaves = jnp.where(y_lo == 0, x_term[1], x_term[0]).astype(BF)
        stays = jnp.where(y_lo == 0, x_term[0], x_term[1])
        w_grad = (stays + lax.ppermute(leaves, DP, YLO_SWAP).astype(F32)).astype(BF)

    with jax.named_scope("sum_over_z"):
        exchange = lambda pair: lax.all_to_all(
            pair, MP, 0, 0, axis_index_groups=SAME_YHI, tiled=True
        )
        sum_a = jnp.sum(exchange(pair_a).astype(F32), axis=0)
        sum_b = jnp.sum(exchange(pair_b).astype(F32), axis=0)
        dnormed = jnp.concatenate([sum_a, sum_b[:share]], axis=1)
        sums = unpack(sum_b[share:])
        plain = jnp.concatenate([sums[0:1], sums[4:5]], axis=1)
        cross = jnp.concatenate([sums[1:2], sums[5:6]], axis=1)

    with jax.named_scope("input_gradient"):
        start = mp * share
        xhat_share = lax.dynamic_slice_in_dim(xhat, start, share, 1).T
        gain_share = lax.dynamic_slice_in_dim(layer_norm_gain, start, share, 0)
        input_gradient_rows = (
            (dnormed * gain_share[:, None] - plain / width - xhat_share * (cross / width))
            * inverse.T
        ).T.astype(BF)
        gain_portion = jnp.sum(dnormed * xhat_share, axis=1)

    with jax.named_scope("gain_gradients"):
        small = jnp.concatenate(
            [
                jnp.pad(gain_portion, (0, 128 - share))[None],
                q_part,
                k_part,
                jnp.zeros((5, 128), F32),
            ],
            axis=0,
        )
        copies = jnp.broadcast_to(small[None], (NX * NYL * NC, 8, 128))
        summed = jnp.sum(lax.all_to_all(copies, DP, 0, 0, tiled=True), axis=0)
    return (
        context,
        input_gradient_rows,
        summed[0, :share],
        w_grad,
        summed[1:2],
        summed[2:3],
    )


def solution(mesh):
    placed = (P("dp", None), P(), P("dp", "mp"), P("mp", None), P("mp", None), P("dp", "mp"))
    return jax.shard_map(
        per_device,
        mesh=mesh,
        in_specs=placed,
        out_specs=(
            P("dp", "mp"),
            P("dp", "mp"),
            P("mp"),
            P("dp", "mp"),
            P("mp", None),
            P("mp", None),
        ),
        check_vma=False,
    )
```

```python
import jax
import jax.numpy as jnp
from jax import lax
from jax.sharding import PartitionSpec as P

BF = jnp.bfloat16
F32 = jnp.float32
PATCHES = 256
DP, MP = "dp", "mp"
NX, NYL, NC = 4, 2, 2
NZ, NYH = 16, 2

CORE_SWAP = [(i, i ^ 1) for i in range(NX * NYL * NC)]
SAME_CORE = [[2 * i + c for i in range(NX * NYL)] for c in range(NC)]
YLO_SWAP = [(i, i ^ 2) for i in range(NX * NYL * NC)]
X_STEPS = [
    [(i, (i + step * NYL * NC) % (NX * NYL * NC)) for i in range(NX * NYL * NC)]
    for step in range(1, NX)
]
NEAR = [[2 * z + j for j in range(2 * NYH)] for z in range(0, NZ, 2)]
FAR = [[2 * NYH * k + j for k in range(NZ // 2)] for j in range(2 * NYH)]


def head_norm(raw):
    centered = raw - jnp.mean(raw, axis=-1, keepdims=True)
    inverse = lax.rsqrt(jnp.mean(centered * centered, axis=-1, keepdims=True) + 1e-06)
    return centered * inverse, inverse


def norm_backward_pass(grad_hat, normal, inverse):
    first = jnp.mean(grad_hat, axis=-1, keepdims=True)
    second = jnp.mean(grad_hat * normal, axis=-1, keepdims=True)
    return (grad_hat - first - normal * second) * inverse


def dot(a, b, ca, cb):
    return lax.dot_general(a, b, (((ca,), (cb,)), ((), ())), preferred_element_type=F32)


def attend(raw, grad, q_gain, k_gain):
    hd = q_gain.shape[-1]
    scale = hd ** (-0.5)
    qhat, q_inv = head_norm(raw[:, :hd])
    khat, k_inv = head_norm(raw[:, hd : 2 * hd])
    value = raw[:, 2 * hd :].astype(BF)
    q_norm = (qhat * q_gain).astype(BF)
    k_norm = (khat * k_gain).astype(BF)
    expo = jnp.exp(dot(q_norm, k_norm, 1, 1) * scale)
    probs = expo / jnp.sum(expo, axis=-1, keepdims=True)
    probs_b = probs.astype(BF)
    context = dot(probs_b, value, 1, 0).astype(BF)
    dprob = dot(grad, value, 1, 1)
    dvalue = dot(probs_b, grad, 0, 0).astype(BF)
    dscore = (probs * (dprob - jnp.sum(probs * dprob, axis=-1, keepdims=True)) * scale).astype(BF)
    dqn = dot(dscore, k_norm, 1, 0)
    dkn = dot(dscore, q_norm, 0, 0)
    q_part = jnp.sum(dqn * qhat, axis=0, keepdims=True)
    k_part = jnp.sum(dkn * khat, axis=0, keepdims=True)
    dquery = norm_backward_pass(dqn * q_gain, qhat, q_inv).astype(BF)
    dkey = norm_backward_pass(dkn * k_gain, khat, k_inv).astype(BF)
    return context, jnp.concatenate([dquery, dkey, dvalue], axis=1), q_part, k_part


def hi_lo(value):
    hi = value.astype(BF)
    lo = (value - hi.astype(F32)).astype(BF)
    return hi, lo


def pack(sums):
    hi, lo = hi_lo(sums)
    row = lax.broadcasted_iota(jnp.int32, sums.shape, 0)
    rows = jnp.where(row % 4 < 2, hi, lo)
    return jnp.concatenate([rows, jnp.zeros_like(rows)], axis=0)


def unpack(got):
    got = got.astype(F32)
    first, second = got[0:2] + got[2:4], got[4:6] + got[6:8]
    return jnp.concatenate([first, first, second, second], axis=0)


def after(value, other):
    first = other.reshape(-1, other.shape[-1])[:1, :128].astype(F32)
    zero = jnp.minimum(jnp.abs(first), 0.0)
    return value + jnp.concatenate([zero] * (value.shape[-1] // 128), axis=1)


def per_device(tokens, layer_norm_gain, w_qkv, q_gain, k_gain, ctx_grad):
    rows, width = tokens.shape
    w_rows, columns = w_qkv.shape
    share = width // (NZ * NYH)
    core = lax.axis_index(DP) % 2
    y_lo = (lax.axis_index(DP) // NC) % NYL
    x_at = lax.axis_index(DP) // (NYL * NC)
    mp = lax.axis_index(MP)
    lane = rows // 2

    with jax.named_scope("gather_w"):
        copies = jnp.broadcast_to(w_qkv[None], (NX * NYL, w_rows, columns))
        own = lax.all_to_all(copies, DP, 0, 0, axis_index_groups=SAME_CORE, tiled=True)
        other = lax.ppermute(own, DP, CORE_SWAP)
        full = jnp.stack(
            [jnp.where(core == 0, own, other), jnp.where(core == 0, other, own)], axis=1
        ).reshape(width, columns)

    with jax.named_scope("input_norm"):
        x_float = tokens.astype(F32)
        centered = x_float - jnp.mean(x_float, axis=-1, keepdims=True)
        inverse = lax.rsqrt(jnp.mean(centered * centered, axis=-1, keepdims=True) + 1e-06)
        xhat = centered * inverse
        normed = (xhat * layer_norm_gain).astype(BF)

    with jax.named_scope("attention"):
        qkv = dot(normed, full, 1, 0)
        context, dqkv, q_part, k_part = attend(qkv, ctx_grad, q_gain, k_gain)

    with jax.named_scope("patch_sums"):
        weighted = jnp.sum(full.astype(F32) * layer_norm_gain[:, None], axis=0, keepdims=True)
        row = lax.broadcasted_iota(jnp.int32, (8, columns), 0)
        w_hi, w_lo = hi_lo(jnp.where(row % 2 == 0, weighted, 0.0))
        ones = (row % 2 == 1).astype(BF)
        p_hi, p_lo = hi_lo(dqkv.astype(F32) * qkv)
        sums = (dot(w_hi, dqkv, 1, 1) + dot(w_lo, dqkv, 1, 1)) + (
            dot(ones, p_hi, 1, 1) + dot(ones, p_lo, 1, 1)
        )
        sums = jnp.concatenate([sums[:4, :lane], sums[:4, lane:]], axis=0)

    with jax.named_scope("input_gradient_partial"):
        chunk = 2 * share
        part = dot(full, dqkv, 1, 1).astype(BF)
        part = part.reshape(NZ // 2, 2 * NYH, share, 2, lane)
        part = part.transpose(1, 0, 3, 2, 4).reshape(2 * NYH, NZ // 2 * chunk, lane)
        riding = jnp.broadcast_to(pack(sums)[None], (2 * NYH, 16, lane))
        part = jnp.concatenate([part, riding], axis=1)
        near = lax.all_to_all(part, MP, 0, 0, axis_index_groups=NEAR, tiled=True)

    with jax.named_scope("w_grad"):
        term = after(dot(normed, dqkv, 0, 0), part)
        term = term.astype(BF).reshape(NX * NYL, NC, w_rows, columns)
        term_keep = jnp.where(core == 0, term[:, 0], term[:, 1])
        term_send = jnp.where(core == 0, term[:, 1], term[:, 0])
        term_got = lax.ppermute(term_send, DP, CORE_SWAP)
        chip = (term_keep.astype(F32) + term_got.astype(F32)).astype(BF)
        chip = chip.reshape(NX, NYL, w_rows, columns)
        x_term = lax.dynamic_index_in_dim(chip, x_at, 0, False).astype(F32)
        for step, pairs in enumerate(X_STEPS, 1):
            leaves = lax.dynamic_index_in_dim(chip, (x_at + step) % NX, 0, False)
            x_term = x_term + lax.ppermute(leaves, DP, pairs).astype(F32)

    with jax.named_scope("sum_over_near"):
        many = NZ // 2 * chunk
        pair = jnp.sum(near[:, :many].astype(F32), axis=0)
        pair = after(pair, chip).astype(BF).reshape(NZ // 2, chunk, lane)
        sums = near[:, many:].astype(F32)
        sums = unpack(sums[0]) + unpack(sums[1]) + unpack(sums[2]) + unpack(sums[3])
        riding = jnp.broadcast_to(pack(sums)[None], (NZ // 2, 16, lane))
        pair = jnp.concatenate([pair, riding], axis=1)
        far = lax.all_to_all(pair, MP, 0, 0, axis_index_groups=FAR, tiled=True)

    with jax.named_scope("w_grad_y"):
        x_term = after(x_term, pair)
        leaves = jnp.where(y_lo == 0, x_term[1], x_term[0]).astype(BF)
        stays = jnp.where(y_lo == 0, x_term[0], x_term[1])
        w_grad = (stays + lax.ppermute(leaves, DP, YLO_SWAP).astype(F32)).astype(BF)

    with jax.named_scope("sum_over_far"):
        total = jnp.sum(far.astype(F32), axis=0)
        dnormed = jnp.concatenate([total[:share], total[share:chunk]], axis=1)
        sums = unpack(total[chunk:])
        plain = jnp.concatenate([sums[0:1], sums[4:5]], axis=1)
        cross = jnp.concatenate([sums[1:2], sums[5:6]], axis=1)

    with jax.named_scope("input_gradient"):
        start = mp * share
        xhat_share = lax.dynamic_slice_in_dim(xhat, start, share, 1).T
        gain_share = lax.dynamic_slice_in_dim(layer_norm_gain, start, share, 0)
        input_gradient_rows = (
            (dnormed * gain_share[:, None] - plain / width - xhat_share * (cross / width))
            * inverse.T
        ).T.astype(BF)
        gain_portion = jnp.sum(dnormed * xhat_share, axis=1)

    with jax.named_scope("gain_gradients"):
        small = jnp.concatenate(
            [
                jnp.pad(gain_portion, (0, 128 - share))[None],
                q_part,
                k_part,
                jnp.zeros((5, 128), F32),
            ],
            axis=0,
        )
        copies = jnp.broadcast_to(small[None], (NX * NYL * NC, 8, 128))
        summed = jnp.sum(lax.all_to_all(copies, DP, 0, 0, tiled=True), axis=0)
    return (
        context,
        input_gradient_rows,
        summed[0, :share],
        w_grad,
        summed[1:2],
        summed[2:3],
    )


def solution(mesh):
    placed = (P("dp", None), P(), P("dp", "mp"), P("mp", None), P("mp", None), P("dp", "mp"))
    return jax.shard_map(
        per_device,
        mesh=mesh,
        in_specs=placed,
        out_specs=(
            P("dp", "mp"),
            P("dp", "mp"),
            P("mp"),
            P("dp", "mp"),
            P("mp", None),
            P("mp", None),
        ),
        check_vma=False,
    )
```

```python
import jax
import jax.numpy as jnp
from jax import lax
from jax.experimental import pallas as pl
from jax.experimental.pallas import tpu as pltpu
from jax.sharding import PartitionSpec as P

BF = jnp.bfloat16
F32 = jnp.float32
PATCHES = 256
DP, MP = "dp", "mp"
NX, NYL, NC = 4, 2, 2
NZ, NYH = 16, 2

CORE_SWAP = [(i, i ^ 1) for i in range(NX * NYL * NC)]
SAME_CORE = [[2 * i + c for i in range(NX * NYL)] for c in range(NC)]
YLO_SWAP = [(i, i ^ 2) for i in range(NX * NYL * NC)]
X_STEPS = [
    [(i, (i + step * NYL * NC) % (NX * NYL * NC)) for i in range(NX * NYL * NC)]
    for step in range(1, NX)
]
NEAR = [[2 * z + j for j in range(2 * NYH)] for z in range(0, NZ, 2)]
FAR = [[2 * NYH * k + j for k in range(NZ // 2)] for j in range(2 * NYH)]


def head_norm(raw):
    centered = raw - jnp.mean(raw, axis=-1, keepdims=True)
    inverse = lax.rsqrt(jnp.mean(centered * centered, axis=-1, keepdims=True) + 1e-06)
    return centered * inverse, inverse


def norm_backward_pass(grad_hat, normal, inverse):
    first = jnp.mean(grad_hat, axis=-1, keepdims=True)
    second = jnp.mean(grad_hat * normal, axis=-1, keepdims=True)
    return (grad_hat - first - normal * second) * inverse


def dot(a, b, ca, cb):
    return lax.dot_general(a, b, (((ca,), (cb,)), ((), ())), preferred_element_type=F32)


def hi_lo(value):
    hi = value.astype(BF)
    lo = (value - hi.astype(F32)).astype(BF)
    return hi, lo


def pack(sums):
    hi = sums.astype(BF).astype(F32)
    row = lax.broadcasted_iota(jnp.int32, sums.shape, 0)
    return jnp.where(row % 4 < 2, hi, sums - hi).astype(BF)


def unpack(got):
    first, second = got[0:2] + got[2:4], got[8:10] + got[10:12]
    return jnp.concatenate([first] * 4 + [second] * 4, axis=0)


def after(value, other):
    first = other.reshape(-1, other.shape[-1])[:1, :128].astype(F32)
    zero = jnp.minimum(jnp.abs(first), 0.0)
    return value + jnp.concatenate([zero] * (value.shape[-1] // 128), axis=1)


def head_kernel(
    core_ref, x_ref, own_ref, other_ref, grad_ref, q_gain_ref, k_gain_ref,
    context_ref, dqkv_ref, part_ref, gains_ref, full_ref,
):
    rows, hd = grad_ref.shape
    lane = rows // 2
    blocks, w_rows, columns = own_ref.shape
    share = w_rows // 2
    own_first = core_ref[0] == 0
    for at in range(blocks):
        own, other = own_ref[at], other_ref[at]
        full_ref[2 * at] = jnp.where(own_first, own, other)
        full_ref[2 * at + 1] = jnp.where(own_first, other, own)
    full = full_ref[...].reshape(2 * blocks * w_rows, columns)
    product = dot(x_ref[...], full, 1, 0)
    raw = product[:rows]
    weighted = product[rows : rows + 1] + product[rows + 1 : rows + 2]

    q_gain, k_gain, grad = q_gain_ref[...], k_gain_ref[...], grad_ref[...]
    scale = hd ** (-0.5)
    qhat, q_inv = head_norm(raw[:, :hd])
    khat, k_inv = head_norm(raw[:, hd : 2 * hd])
    value = raw[:, 2 * hd :].astype(BF)
    q_norm = (qhat * q_gain).astype(BF)
    k_norm = (khat * k_gain).astype(BF)
    expo = jnp.exp(dot(q_norm, k_norm, 1, 1) * scale)
    probs = expo / jnp.sum(expo, axis=-1, keepdims=True)
    probs_b = probs.astype(BF)
    context_ref[...] = dot(probs_b, value, 1, 0).astype(BF)
    dprob = dot(grad, value, 1, 1)
    dscore = (probs * (dprob - jnp.sum(probs * dprob, axis=-1, keepdims=True)) * scale).astype(BF)
    dqn = dot(dscore, k_norm, 1, 0)
    dkn = dot(dscore, q_norm, 0, 0)
    gains_ref[0:1] = jnp.sum(dqn * qhat, axis=0, keepdims=True)
    gains_ref[1:2] = jnp.sum(dkn * khat, axis=0, keepdims=True)
    gains_ref[2:] = jnp.zeros((gains_ref.shape[0] - 2, hd), F32)
    dqkv = jnp.concatenate(
        [
            norm_backward_pass(dqn * q_gain, qhat, q_inv).astype(BF),
            norm_backward_pass(dkn * k_gain, khat, k_inv).astype(BF),
            dot(probs_b, grad, 0, 0).astype(BF),
        ],
        axis=1,
    )
    dqkv_ref[...] = dqkv

    for k in range(blocks):
        pair = full_ref[2 * k : 2 * k + 2].reshape(2 * w_rows, columns)
        part = dot(pair, dqkv, 1, 1).astype(BF)
        for group in range(4):
            for half in range(2):
                at = (2 * k + half) * share
                part_ref[group, at : at + share] = part[
                    group * share : (group + 1) * share, half * lane : (half + 1) * lane
                ]

    row = lax.broadcasted_iota(jnp.int32, (8, columns), 0)
    w_hi, w_lo = hi_lo(jnp.where(row % 2 == 0, weighted, 0.0))
    ones = jnp.where(row % 2 == 1, 1.0, 0.0).astype(BF)
    p_hi, p_lo = hi_lo(dqkv.astype(F32) * raw)
    sums = (dot(w_hi, dqkv, 1, 1) + dot(w_lo, dqkv, 1, 1)) + (
        dot(ones, p_hi, 1, 1) + dot(ones, p_lo, 1, 1)
    )
    packed = pack(jnp.concatenate([sums[:, :lane], sums[:, lane:]], axis=0))
    for group in range(4):
        part_ref[group, 2 * blocks * share :] = packed


def run_head(core, x, own, other, grad, q_gain, k_gain):
    rows, hd = grad.shape
    blocks, w_rows, columns = own.shape
    vmem = pl.BlockSpec(memory_space=pltpu.VMEM)
    return pl.pallas_call(
        head_kernel,
        in_specs=[pl.BlockSpec(memory_space=pltpu.SMEM)] + [vmem] * 6,
        out_specs=[vmem] * 4,
        out_shape=[
            jax.ShapeDtypeStruct((rows, hd), BF),
            jax.ShapeDtypeStruct((rows, columns), BF),
            jax.ShapeDtypeStruct((4, blocks * w_rows + 16, rows // 2), BF),
            jax.ShapeDtypeStruct((8, hd), F32),
        ],
        scratch_shapes=[pltpu.VMEM((2 * blocks, w_rows, columns), BF)],
        compiler_params=pltpu.CompilerParams(vmem_limit_bytes=48 * 2**20),
        cost_estimate=pl.CostEstimate(
            flops=1_400_000_000, bytes_accessed=9_000_000, transcendentals=65536
        ),
    )(core.reshape(1), x, own, other, grad, q_gain, k_gain)


def per_device(tokens, layer_norm_gain, w_qkv, q_gain, k_gain, ctx_grad):
    rows, width = tokens.shape
    w_rows, columns = w_qkv.shape
    share = width // (NZ * NYH)
    core = lax.axis_index(DP) % 2
    y_lo = (lax.axis_index(DP) // NC) % NYL
    x_at = lax.axis_index(DP) // (NYL * NC)
    mp = lax.axis_index(MP)
    lane = rows // 2

    with jax.named_scope("gather_w"):
        copies = jnp.broadcast_to(w_qkv[None], (NX * NYL, w_rows, columns))
        own = lax.all_to_all(copies, DP, 0, 0, axis_index_groups=SAME_CORE, tiled=True)
        other = lax.ppermute(own, DP, CORE_SWAP)

    with jax.named_scope("input_norm"):
        x_float = tokens.astype(F32)
        centered = x_float - jnp.mean(x_float, axis=-1, keepdims=True)
        inverse = lax.rsqrt(jnp.mean(centered * centered, axis=-1, keepdims=True) + 1e-06)
        xhat = centered * inverse
        normed = (xhat * layer_norm_gain).astype(BF)

        extra = jnp.concatenate(
            [jnp.stack(hi_lo(layer_norm_gain)), jnp.zeros((14, width), BF)], axis=0
        )
        lhs = jnp.concatenate([normed, extra], axis=0)

    with jax.named_scope("head"):
        context, dqkv, part, head_gains = run_head(
            core, lhs, own, other, ctx_grad, q_gain, k_gain
        )

    with jax.named_scope("input_gradient_near"):
        chunk = 2 * share
        near = lax.all_to_all(part, MP, 0, 0, axis_index_groups=NEAR, tiled=True)

    with jax.named_scope("w_grad"):
        term = dot(normed, dqkv, 0, 0).astype(BF).reshape(NX * NYL, NC, w_rows, columns)
        term_keep = jnp.where(core == 0, term[:, 0], term[:, 1])
        term_send = jnp.where(core == 0, term[:, 1], term[:, 0])
        term_got = lax.ppermute(term_send, DP, CORE_SWAP)
        chip = (term_keep.astype(F32) + term_got.astype(F32)).astype(BF)
        chip = chip.reshape(NX, NYL, w_rows, columns)
        x_term = lax.dynamic_index_in_dim(chip, x_at, 0, False).astype(F32)
        for step, pairs in enumerate(X_STEPS, 1):
            leaves = lax.dynamic_index_in_dim(chip, (x_at + step) % NX, 0, False)
            x_term = x_term + lax.ppermute(leaves, DP, pairs).astype(F32)

    with jax.named_scope("sum_over_near"):
        many = NZ // 2 * chunk
        pair = jnp.sum(near[:, :many].astype(F32), axis=0)
        pair = after(pair, x_term).astype(BF).reshape(NZ // 2, chunk, lane)
        sums = unpack(jnp.sum(near[:, many:].astype(F32), axis=0))
        riding = jnp.broadcast_to(pack(sums)[None], (NZ // 2, 16, lane))
        pair = jnp.concatenate([pair, riding], axis=1)
        far = lax.all_to_all(pair, MP, 0, 0, axis_index_groups=FAR, tiled=True)

    with jax.named_scope("w_grad_y"):
        x_term = after(x_term, pair)
        leaves = jnp.where(y_lo == 0, x_term[1], x_term[0]).astype(BF)
        stays = jnp.where(y_lo == 0, x_term[0], x_term[1])
        w_grad = (stays + lax.ppermute(leaves, DP, YLO_SWAP).astype(F32)).astype(BF)

    with jax.named_scope("sum_over_far"):
        total = jnp.sum(far.astype(F32), axis=0)
        dnormed = jnp.concatenate([total[:share], total[share:chunk]], axis=1)
        sums = unpack(total[chunk:])
        plain = jnp.concatenate([sums[0:1], sums[8:9]], axis=1)
        cross = jnp.concatenate([sums[1:2], sums[9:10]], axis=1)

    with jax.named_scope("input_gradient"):
        start = mp * share
        xhat_share = lax.dynamic_slice_in_dim(xhat, start, share, 1).T
        gain_share = lax.dynamic_slice_in_dim(layer_norm_gain, start, share, 0)
        input_gradient_rows = (
            (dnormed * gain_share[:, None] - plain / width - xhat_share * (cross / width))
            * inverse.T
        ).T.astype(BF)
        gain_portion = jnp.sum(dnormed * xhat_share, axis=1)

    with jax.named_scope("gain_gradients"):
        portion = jnp.pad(gain_portion, (0, 128 - share))[None]
        small = jnp.concatenate([head_gains[:7], portion], axis=0)
        copies = jnp.broadcast_to(small[None], (NX * NYL * NC, 8, 128))
        summed = jnp.sum(lax.all_to_all(copies, DP, 0, 0, tiled=True), axis=0)
    return (
        context,
        input_gradient_rows,
        summed[7, :share],
        w_grad,
        summed[0:1],
        summed[1:2],
    )


def solution(mesh):
    placed = (P("dp", None), P(), P("dp", "mp"), P("mp", None), P("mp", None), P("dp", "mp"))
    return jax.shard_map(
        per_device,
        mesh=mesh,
        in_specs=placed,
        out_specs=(
            P("dp", "mp"),
            P("dp", "mp"),
            P("mp"),
            P("dp", "mp"),
            P("mp", None),
            P("mp", None),
        ),
        check_vma=False,
    )
```

```python
import jax
import jax.numpy as jnp
from jax import lax
from jax.experimental import pallas as pl
from jax.experimental.pallas import tpu as pltpu
from jax.sharding import PartitionSpec as P

BF = jnp.bfloat16
F32 = jnp.float32
PATCHES = 256
DP, MP = "dp", "mp"
NX, NYL, NC = 4, 2, 2
NZ, NYH = 16, 2

CORE_SWAP = [(i, i ^ 1) for i in range(NX * NYL * NC)]
SAME_CORE = [[2 * i + c for i in range(NX * NYL)] for c in range(NC)]
YLO_SWAP = [(i, i ^ 2) for i in range(NX * NYL * NC)]
X_STEPS = [
    [(i, (i + step * NYL * NC) % (NX * NYL * NC)) for i in range(NX * NYL * NC)]
    for step in range(1, NX)
]
NEAR = [[2 * z + j for j in range(2 * NYH)] for z in range(0, NZ, 2)]
FAR = [[2 * NYH * k + j for k in range(NZ // 2)] for j in range(2 * NYH)]


def head_norm(raw):
    centered = raw - jnp.mean(raw, axis=-1, keepdims=True)
    inverse = lax.rsqrt(jnp.mean(centered * centered, axis=-1, keepdims=True) + 1e-06)
    return centered * inverse, inverse


def norm_backward_pass(grad_hat, normal, inverse):
    first = jnp.mean(grad_hat, axis=-1, keepdims=True)
    second = jnp.mean(grad_hat * normal, axis=-1, keepdims=True)
    return (grad_hat - first - normal * second) * inverse


def dot(a, b, ca, cb):
    return lax.dot_general(a, b, (((ca,), (cb,)), ((), ())), preferred_element_type=F32)


def hi_lo(value):
    hi = value.astype(BF)
    lo = (value - hi.astype(F32)).astype(BF)
    return hi, lo


def pack(sums):
    hi = sums.astype(BF).astype(F32)
    row = lax.broadcasted_iota(jnp.int32, sums.shape, 0)
    return jnp.where(row % 4 < 2, hi, sums - hi).astype(BF)


def unpack(got):
    first, second = got[0:2] + got[2:4], got[8:10] + got[10:12]
    return jnp.concatenate([first] * 4 + [second] * 4, axis=0)


def after(value, other):
    first = other.reshape(-1, other.shape[-1])[:1, :128].astype(F32)
    zero = jnp.minimum(jnp.abs(first), 0.0)
    return value + jnp.concatenate([zero] * (value.shape[-1] // 128), axis=1)


def head_kernel(
    core_ref, x_ref, own_ref, other_ref, grad_ref, q_gain_ref, k_gain_ref,
    context_ref, dqkv_ref, part_ref, gains_ref, full_ref,
):
    rows, hd = grad_ref.shape
    lane = rows // 2
    blocks, w_rows, columns = own_ref.shape
    share = w_rows // 2
    own_first = core_ref[0] == 0
    for at in range(blocks):
        own, other = own_ref[at], other_ref[at]
        full_ref[2 * at] = jnp.where(own_first, own, other)
        full_ref[2 * at + 1] = jnp.where(own_first, other, own)
    full = full_ref[...].reshape(2 * blocks * w_rows, columns)
    product = dot(x_ref[...], full, 1, 0)
    raw = product[:rows]
    weighted = product[rows : rows + 1] + product[rows + 1 : rows + 2]

    q_gain, k_gain, grad = q_gain_ref[...], k_gain_ref[...], grad_ref[...]
    scale = hd ** (-0.5)
    qhat, q_inv = head_norm(raw[:, :hd])
    khat, k_inv = head_norm(raw[:, hd : 2 * hd])
    value = raw[:, 2 * hd :].astype(BF)
    q_norm = (qhat * q_gain).astype(BF)
    k_norm = (khat * k_gain).astype(BF)
    expo = jnp.exp(dot(q_norm, k_norm, 1, 1) * scale)
    probs = expo / jnp.sum(expo, axis=-1, keepdims=True)
    probs_b = probs.astype(BF)
    context_ref[...] = dot(probs_b, value, 1, 0).astype(BF)
    dprob = dot(grad, value, 1, 1)
    dscore = (probs * (dprob - jnp.sum(probs * dprob, axis=-1, keepdims=True)) * scale).astype(BF)
    dqn = dot(dscore, k_norm, 1, 0)
    dkn = dot(dscore, q_norm, 0, 0)
    gains_ref[0:1] = jnp.sum(dqn * qhat, axis=0, keepdims=True)
    gains_ref[1:2] = jnp.sum(dkn * khat, axis=0, keepdims=True)
    gains_ref[2:] = jnp.zeros((gains_ref.shape[0] - 2, hd), F32)
    dqkv = jnp.concatenate(
        [
            norm_backward_pass(dqn * q_gain, qhat, q_inv).astype(BF),
            norm_backward_pass(dkn * k_gain, khat, k_inv).astype(BF),
            dot(probs_b, grad, 0, 0).astype(BF),
        ],
        axis=1,
    )
    dqkv_ref[...] = dqkv

    for k in range(blocks):
        pair = full_ref[2 * k : 2 * k + 2].reshape(2 * w_rows, columns)
        part = dot(pair, dqkv, 1, 1).astype(BF)
        for group in range(4):
            for half in range(2):
                at = (2 * k + half) * share
                part_ref[group, at : at + share] = part[
                    group * share : (group + 1) * share, half * lane : (half + 1) * lane
                ]

    row = lax.broadcasted_iota(jnp.int32, (8, columns), 0)
    w_hi, w_lo = hi_lo(jnp.where(row % 2 == 0, weighted, 0.0))
    ones = jnp.where(row % 2 == 1, 1.0, 0.0).astype(BF)
    p_hi, p_lo = hi_lo(dqkv.astype(F32) * raw)
    sums = (dot(w_hi, dqkv, 1, 1) + dot(w_lo, dqkv, 1, 1)) + (
        dot(ones, p_hi, 1, 1) + dot(ones, p_lo, 1, 1)
    )
    packed = pack(jnp.concatenate([sums[:, :lane], sums[:, lane:]], axis=0))
    for group in range(4):
        part_ref[group, 2 * blocks * share :] = packed


def run_head(core, x, own, other, grad, q_gain, k_gain):
    rows, hd = grad.shape
    blocks, w_rows, columns = own.shape
    vmem = pl.BlockSpec(memory_space=pltpu.VMEM)
    return pl.pallas_call(
        head_kernel,
        in_specs=[pl.BlockSpec(memory_space=pltpu.SMEM)] + [vmem] * 6,
        out_specs=[vmem] * 4,
        out_shape=[
            jax.ShapeDtypeStruct((rows, hd), BF),
            jax.ShapeDtypeStruct((rows, columns), BF),
            jax.ShapeDtypeStruct((4, blocks * w_rows + 16, rows // 2), BF),
            jax.ShapeDtypeStruct((8, hd), F32),
        ],
        scratch_shapes=[pltpu.VMEM((2 * blocks, w_rows, columns), BF)],
        compiler_params=pltpu.CompilerParams(vmem_limit_bytes=48 * 2**20),
        cost_estimate=pl.CostEstimate(
            flops=1_400_000_000, bytes_accessed=9_000_000, transcendentals=65536
        ),
    )(core.reshape(1), x, own, other, grad, q_gain, k_gain)


def per_device(tokens, layer_norm_gain, w_qkv, q_gain, k_gain, ctx_grad):
    rows, width = tokens.shape
    w_rows, columns = w_qkv.shape
    share = width // (NZ * NYH)
    core = lax.axis_index(DP) % 2
    y_lo = (lax.axis_index(DP) // NC) % NYL
    x_at = lax.axis_index(DP) // (NYL * NC)
    mp = lax.axis_index(MP)
    lane = rows // 2

    with jax.named_scope("gather_w"):
        copies = jnp.broadcast_to(w_qkv[None], (NX * NYL, w_rows, columns))
        own = lax.all_to_all(copies, DP, 0, 0, axis_index_groups=SAME_CORE, tiled=True)
        other = lax.ppermute(own, DP, CORE_SWAP)

    with jax.named_scope("input_norm"):
        x_float = tokens.astype(F32)
        mean = jnp.mean(x_float, axis=-1, keepdims=True)
        centered = x_float - mean
        inverse = lax.rsqrt(jnp.mean(centered * centered, axis=-1, keepdims=True) + 1e-06)
        normed = (centered * inverse * layer_norm_gain).astype(BF)

        extra = jnp.concatenate(
            [jnp.stack(hi_lo(layer_norm_gain)), jnp.zeros((14, width), BF)], axis=0
        )
        lhs = jnp.concatenate([normed, extra], axis=0)

    with jax.named_scope("head"):
        context, dqkv, part, head_gains = run_head(
            core, lhs, own, other, ctx_grad, q_gain, k_gain
        )

    with jax.named_scope("input_gradient_near"):
        chunk = 2 * share
        near = lax.all_to_all(part, MP, 0, 0, axis_index_groups=NEAR, tiled=True)

    with jax.named_scope("w_grad"):
        term = dot(normed, dqkv, 0, 0).astype(BF).reshape(NX * NYL, NC, w_rows, columns)
        term_keep = jnp.where(core == 0, term[:, 0], term[:, 1])
        term_send = jnp.where(core == 0, term[:, 1], term[:, 0])
        term_got = lax.ppermute(term_send, DP, CORE_SWAP)
        chip = (term_keep.astype(F32) + term_got.astype(F32)).astype(BF)
        chip = chip.reshape(NX, NYL, w_rows, columns)
        x_term = lax.dynamic_index_in_dim(chip, x_at, 0, False).astype(F32)
        for step, pairs in enumerate(X_STEPS, 1):
            leaves = lax.dynamic_index_in_dim(chip, (x_at + step) % NX, 0, False)
            x_term = x_term + lax.ppermute(leaves, DP, pairs).astype(F32)

    with jax.named_scope("sum_over_near"):
        many = NZ // 2 * chunk
        pair = jnp.sum(near[:, :many].astype(F32), axis=0)
        pair = after(pair, chip).astype(BF).reshape(NZ // 2, chunk, lane)
        sums = unpack(jnp.sum(near[:, many:].astype(F32), axis=0))
        riding = jnp.broadcast_to(pack(sums)[None], (NZ // 2, 16, lane))
        pair = jnp.concatenate([pair, riding], axis=1)
        far = lax.all_to_all(pair, MP, 0, 0, axis_index_groups=FAR, tiled=True)

    with jax.named_scope("w_grad_y"):
        x_term = after(x_term, pair)
        leaves = jnp.where(y_lo == 0, x_term[1], x_term[0]).astype(BF)
        stays = jnp.where(y_lo == 0, x_term[0], x_term[1])
        w_grad = (stays + lax.ppermute(leaves, DP, YLO_SWAP).astype(F32)).astype(BF)

    with jax.named_scope("sum_over_far"):
        total = jnp.sum(far.astype(F32), axis=0)
        dnormed = jnp.concatenate([total[:share], total[share:chunk]], axis=1)
        sums = unpack(total[chunk:])
        plain = jnp.concatenate([sums[0:1], sums[8:9]], axis=1)
        cross = jnp.concatenate([sums[1:2], sums[9:10]], axis=1)

    with jax.named_scope("input_gradient"):
        start = mp * share
        tokens_share = lax.dynamic_slice_in_dim(tokens, start, share, 1).astype(F32)
        xhat_share = ((tokens_share - mean) * inverse).T
        gain_share = lax.dynamic_slice_in_dim(layer_norm_gain, start, share, 0)
        input_gradient_rows = (
            (dnormed * gain_share[:, None] - plain / width - xhat_share * (cross / width))
            * inverse.T
        ).T.astype(BF)
        gain_portion = jnp.sum(dnormed * xhat_share, axis=1)

    with jax.named_scope("gain_gradients"):
        portion = jnp.pad(gain_portion, (0, 128 - share))[None]
        small = jnp.concatenate([head_gains[:7], portion], axis=0)
        copies = jnp.broadcast_to(small[None], (NX * NYL * NC, 8, 128))
        summed = jnp.sum(lax.all_to_all(copies, DP, 0, 0, tiled=True), axis=0)
    return (
        context,
        input_gradient_rows,
        summed[7, :share],
        w_grad,
        summed[0:1],
        summed[1:2],
    )


def solution(mesh):
    placed = (P("dp", None), P(), P("dp", "mp"), P("mp", None), P("mp", None), P("dp", "mp"))
    return jax.shard_map(
        per_device,
        mesh=mesh,
        in_specs=placed,
        out_specs=(
            P("dp", "mp"),
            P("dp", "mp"),
            P("mp"),
            P("dp", "mp"),
            P("mp", None),
            P("mp", None),
        ),
        check_vma=False,
    )
```

```python
import functools

import jax
import jax.numpy as jnp
from jax import lax
from jax.experimental import pallas as pl
from jax.experimental.pallas import tpu as pltpu
from jax.sharding import PartitionSpec as P

BF = jnp.bfloat16
F32 = jnp.float32
PATCHES = 256
DP, MP = "dp", "mp"
NX, NYL, NC = 4, 2, 2
NZ, NYH = 16, 2

CORE_SWAP = [(i, i ^ 1) for i in range(NX * NYL * NC)]
SAME_CORE = [[2 * i + c for i in range(NX * NYL)] for c in range(NC)]
YLO_SWAP = [(i, i ^ 2) for i in range(NX * NYL * NC)]
X_STEPS = [
    [(i, (i + step * NYL * NC) % (NX * NYL * NC)) for i in range(NX * NYL * NC)]
    for step in range(1, NX)
]
NEAR = [[2 * z + j for j in range(2 * NYH)] for z in range(0, NZ, 2)]
FAR = [[2 * NYH * k + j for k in range(NZ // 2)] for j in range(2 * NYH)]


def head_norm(raw):
    centered = raw - jnp.mean(raw, axis=-1, keepdims=True)
    inverse = lax.rsqrt(jnp.mean(centered * centered, axis=-1, keepdims=True) + 1e-06)
    return centered * inverse, inverse


def norm_backward_pass(grad_hat, normal, inverse):
    first = jnp.mean(grad_hat, axis=-1, keepdims=True)
    second = jnp.mean(grad_hat * normal, axis=-1, keepdims=True)
    return (grad_hat - first - normal * second) * inverse


def dot(a, b, ca, cb):
    return lax.dot_general(a, b, (((ca,), (cb,)), ((), ())), preferred_element_type=F32)


def hi_lo(value):
    hi = value.astype(BF)
    lo = (value - hi.astype(F32)).astype(BF)
    return hi, lo


def pack(sums):
    hi = sums.astype(BF).astype(F32)
    row = lax.broadcasted_iota(jnp.int32, sums.shape, 0)
    return jnp.where(row % 4 < 2, hi, sums - hi).astype(BF)


def head_kernel(
    core_ref, x_ref, own_ref, other_ref, grad_ref, q_gain_ref, k_gain_ref,
    context_ref, dqkv_ref, part_ref, gains_ref, full_ref,
):
    rows, hd = grad_ref.shape
    lane = rows // 2
    blocks, w_rows, columns = own_ref.shape
    share = w_rows // 2
    own_first = core_ref[0] == 0
    for at in range(blocks):
        own, other = own_ref[at], other_ref[at]
        full_ref[2 * at] = jnp.where(own_first, own, other)
        full_ref[2 * at + 1] = jnp.where(own_first, other, own)
    full = full_ref[...].reshape(2 * blocks * w_rows, columns)
    product = dot(x_ref[...], full, 1, 0)
    raw = product[:rows]
    weighted = product[rows : rows + 1] + product[rows + 1 : rows + 2]

    q_gain, k_gain, grad = q_gain_ref[...], k_gain_ref[...], grad_ref[...]
    scale = hd ** (-0.5)
    qhat, q_inv = head_norm(raw[:, :hd])
    khat, k_inv = head_norm(raw[:, hd : 2 * hd])
    value = raw[:, 2 * hd :].astype(BF)
    q_norm = (qhat * q_gain).astype(BF)
    k_norm = (khat * k_gain).astype(BF)
    expo = jnp.exp(dot(q_norm, k_norm, 1, 1) * scale)
    probs = expo / jnp.sum(expo, axis=-1, keepdims=True)
    probs_b = probs.astype(BF)
    context_ref[...] = dot(probs_b, value, 1, 0).astype(BF)
    dprob = dot(grad, value, 1, 1)
    dscore = (probs * (dprob - jnp.sum(probs * dprob, axis=-1, keepdims=True)) * scale).astype(BF)
    dqn = dot(dscore, k_norm, 1, 0)
    dkn = dot(dscore, q_norm, 0, 0)
    gains_ref[0:1] = jnp.sum(dqn * qhat, axis=0, keepdims=True)
    gains_ref[1:2] = jnp.sum(dkn * khat, axis=0, keepdims=True)
    gains_ref[2:] = jnp.zeros((gains_ref.shape[0] - 2, hd), F32)
    dqkv = jnp.concatenate(
        [
            norm_backward_pass(dqn * q_gain, qhat, q_inv).astype(BF),
            norm_backward_pass(dkn * k_gain, khat, k_inv).astype(BF),
            dot(probs_b, grad, 0, 0).astype(BF),
        ],
        axis=1,
    )
    dqkv_ref[...] = dqkv

    for k in range(blocks):
        pair = full_ref[2 * k : 2 * k + 2].reshape(2 * w_rows, columns)
        part = dot(pair, dqkv, 1, 1).astype(BF)
        for group in range(4):
            for half in range(2):
                at = (2 * k + half) * share
                part_ref[group, at : at + share] = part[
                    group * share : (group + 1) * share, half * lane : (half + 1) * lane
                ]

    row = lax.broadcasted_iota(jnp.int32, (8, columns), 0)
    w_hi, w_lo = hi_lo(jnp.where(row % 2 == 0, weighted, 0.0))
    ones = jnp.where(row % 2 == 1, 1.0, 0.0).astype(BF)
    p_hi, p_lo = hi_lo(dqkv.astype(F32) * raw)
    sums = (dot(w_hi, dqkv, 1, 1) + dot(w_lo, dqkv, 1, 1)) + (
        dot(ones, p_hi, 1, 1) + dot(ones, p_lo, 1, 1)
    )
    packed = pack(jnp.concatenate([sums[:, :lane], sums[:, lane:]], axis=0))
    for group in range(4):
        part_ref[group, 2 * blocks * share :] = packed


def run_head(core, x, own, other, grad, q_gain, k_gain):
    rows, hd = grad.shape
    blocks, w_rows, columns = own.shape
    vmem = pl.BlockSpec(memory_space=pltpu.VMEM)
    return pl.pallas_call(
        head_kernel,
        in_specs=[pl.BlockSpec(memory_space=pltpu.SMEM)] + [vmem] * 6,
        out_specs=[vmem] * 4,
        out_shape=[
            jax.ShapeDtypeStruct((rows, hd), BF),
            jax.ShapeDtypeStruct((rows, columns), BF),
            jax.ShapeDtypeStruct((4, blocks * w_rows + 16, rows // 2), BF),
            jax.ShapeDtypeStruct((8, hd), F32),
        ],
        scratch_shapes=[pltpu.VMEM((2 * blocks, w_rows, columns), BF)],
        compiler_params=pltpu.CompilerParams(vmem_limit_bytes=48 * 2**20),
        cost_estimate=pl.CostEstimate(
            flops=1_400_000_000, bytes_accessed=9_000_000, transcendentals=65536
        ),
    )(core.reshape(1), x, own, other, grad, q_gain, k_gain)


def near_kernel(near_ref, *refs):
    out_ref = refs[-1]
    blocks, chunk = out_ref.shape[0], out_ref.shape[1] - 16
    add = lambda at, size: sum(
        near_ref[group, at : at + size].astype(F32) for group in range(near_ref.shape[0])
    )
    got = add(blocks * chunk, 16)
    row = lax.broadcasted_iota(jnp.int32, got.shape, 0)
    both = got + pltpu.roll(got, 14, 0)
    packed = pack(jnp.where(row % 8 < 2, both, pltpu.roll(both, 2, 0)))
    for k in range(blocks):
        out_ref[k, :chunk] = add(k * chunk, chunk).astype(BF)
        out_ref[k, chunk:] = packed


def sum_near(near, order):
    vmem = pl.BlockSpec(memory_space=pltpu.VMEM)
    blocks = NZ // 2
    chunk = (near.shape[1] - 16) // blocks
    return pl.pallas_call(
        near_kernel,
        in_specs=[vmem] + [pl.BlockSpec(memory_space=pl.ANY)] * len(order),
        out_specs=vmem,
        out_shape=jax.ShapeDtypeStruct((blocks, chunk + 16, near.shape[2]), BF),
        compiler_params=pltpu.CompilerParams(vmem_limit_bytes=24 * 2**20),
    )(near, *order)


def far_kernel(width, far_ref, xhat_ref, gain_ref, inverse_ref, heads_ref, rows_ref, small_ref):
    share = xhat_ref.shape[0]
    lane = far_ref.shape[2]
    total = sum(far_ref[k].astype(F32) for k in range(far_ref.shape[0]))
    last = 2 * share
    product = jnp.zeros((share, lane), F32)
    for half in range(2):
        at = slice(half * lane, (half + 1) * lane)
        dnormed = total[half * share : (half + 1) * share]
        sums = total[last + 8 * half : last + 8 * half + 8]
        plain = sums[0:1] + sums[2:3]
        cross = sums[1:2] + sums[3:4]
        xhat = xhat_ref[:, at]
        rows_ref[:, at] = (
            (dnormed * gain_ref[...] - plain / width - xhat * (cross / width))
            * inverse_ref[:, at]
        ).astype(BF)
        product = product + dnormed * xhat
    small_ref[0] = heads_ref[...]
    small_ref[0, 7:8, :share] = jnp.sum(product.T, axis=0, keepdims=True)
    small = small_ref[0]
    for at in range(1, small_ref.shape[0]):
        small_ref[at] = small


def finish(width, far, xhat, gain, inverse, head_gains):
    vmem = pl.BlockSpec(memory_space=pltpu.VMEM)
    return pl.pallas_call(
        functools.partial(far_kernel, width),
        in_specs=[vmem] * 5,
        out_specs=[vmem] * 2,
        out_shape=[
            jax.ShapeDtypeStruct(xhat.shape, BF),
            jax.ShapeDtypeStruct((NX * NYL * NC,) + head_gains.shape, F32),
        ],
        compiler_params=pltpu.CompilerParams(vmem_limit_bytes=24 * 2**20),
    )(far, xhat, gain, inverse, head_gains)


def per_device(tokens, layer_norm_gain, w_qkv, q_gain, k_gain, ctx_grad):
    rows, width = tokens.shape
    w_rows, columns = w_qkv.shape
    share = width // (NZ * NYH)
    core = lax.axis_index(DP) % 2
    y_lo = (lax.axis_index(DP) // NC) % NYL
    x_at = lax.axis_index(DP) // (NYL * NC)
    mp = lax.axis_index(MP)
    lane = rows // 2

    with jax.named_scope("gather_w"):
        copies = jnp.broadcast_to(w_qkv[None], (NX * NYL, w_rows, columns))
        own = lax.all_to_all(copies, DP, 0, 0, axis_index_groups=SAME_CORE, tiled=True)
        other = lax.ppermute(own, DP, CORE_SWAP)

    with jax.named_scope("input_norm"):
        x_float = tokens.astype(F32)
        mean = jnp.mean(x_float, axis=-1, keepdims=True)
        centered = x_float - mean
        inverse = lax.rsqrt(jnp.mean(centered * centered, axis=-1, keepdims=True) + 1e-06)
        normed = (centered * inverse * layer_norm_gain).astype(BF)

        extra = jnp.concatenate(
            [jnp.stack(hi_lo(layer_norm_gain)), jnp.zeros((14, width), BF)], axis=0
        )
        lhs = jnp.concatenate([normed, extra], axis=0)

    with jax.named_scope("head"):
        context, dqkv, part, head_gains = run_head(
            core, lhs, own, other, ctx_grad, q_gain, k_gain
        )

    with jax.named_scope("input_gradient_near"):
        near = lax.all_to_all(part, MP, 0, 0, axis_index_groups=NEAR, tiled=True)

    with jax.named_scope("w_grad"):
        term = dot(normed, dqkv, 0, 0).astype(BF).reshape(NX * NYL, NC, w_rows, columns)
        term_keep = jnp.where(core == 0, term[:, 0], term[:, 1])
        term_send = jnp.where(core == 0, term[:, 1], term[:, 0])
        term_got = lax.ppermute(term_send, DP, CORE_SWAP)
        chip = (term_keep.astype(F32) + term_got.astype(F32)).astype(BF)
        chip = chip.reshape(NX, NYL, w_rows, columns)
        x_term = lax.dynamic_index_in_dim(chip, x_at, 0, False).astype(F32)
        x_got = [
            lax.ppermute(
                lax.dynamic_index_in_dim(chip, (x_at + step) % NX, 0, False), DP, pairs
            )
            for step, pairs in enumerate(X_STEPS, 1)
        ]

    with jax.named_scope("sum_over_near"):
        pair = sum_near(near, [x_got[0], x_got[2]])
        far = lax.all_to_all(pair, MP, 0, 0, axis_index_groups=FAR, tiled=True)

    with jax.named_scope("w_grad_y"):
        x_term = x_term + sum(got.astype(F32) for got in x_got)
        leaves = jnp.where(y_lo == 0, x_term[1], x_term[0]).astype(BF)
        stays = jnp.where(y_lo == 0, x_term[0], x_term[1])
        w_grad = (stays + lax.ppermute(leaves, DP, YLO_SWAP).astype(F32)).astype(BF)

    with jax.named_scope("input_gradient"):
        start = mp * share
        tokens_share = lax.dynamic_slice_in_dim(tokens, start, share, 1).astype(F32)
        xhat_share = ((tokens_share - mean) * inverse).T
        gain_share = lax.dynamic_slice_in_dim(layer_norm_gain, start, share, 0)
        gradient, copies = finish(
            width, far, xhat_share, gain_share[:, None], inverse.T, head_gains
        )

    with jax.named_scope("gain_gradients"):
        summed = jnp.sum(lax.all_to_all(copies, DP, 0, 0, tiled=True), axis=0)
    return (
        context,
        gradient.T,
        summed[7, :share],
        w_grad,
        summed[0:1],
        summed[1:2],
    )


def solution(mesh):
    placed = (P("dp", None), P(), P("dp", "mp"), P("mp", None), P("mp", None), P("dp", "mp"))
    return jax.shard_map(
        per_device,
        mesh=mesh,
        in_specs=placed,
        out_specs=(
            P("dp", "mp"),
            P("dp", "mp"),
            P("mp"),
            P("dp", "mp"),
            P("mp", None),
            P("mp", None),
        ),
        check_vma=False,
    )
```

```python
import functools

import jax
import jax.numpy as jnp
from jax import lax
from jax.experimental import pallas as pl
from jax.experimental.pallas import tpu as pltpu
from jax.sharding import PartitionSpec as P

BF = jnp.bfloat16
F32 = jnp.float32
PATCHES = 256
DP, MP = "dp", "mp"
NX, NYL, NC = 4, 2, 2
NZ, NYH = 16, 2

CORE_SWAP = [(i, i ^ 1) for i in range(NX * NYL * NC)]
SAME_CORE = [[2 * i + c for i in range(NX * NYL)] for c in range(NC)]
YLO_SWAP = [(i, i ^ 2) for i in range(NX * NYL * NC)]
X_STEPS = [
    [(i, (i + step * NYL * NC) % (NX * NYL * NC)) for i in range(NX * NYL * NC)]
    for step in range(1, NX)
]
NEAR = [[2 * z + j for j in range(2 * NYH)] for z in range(0, NZ, 2)]
FAR = [[2 * NYH * k + j for k in range(NZ // 2)] for j in range(2 * NYH)]


def head_norm(raw):
    centered = raw - jnp.mean(raw, axis=-1, keepdims=True)
    inverse = lax.rsqrt(jnp.mean(centered * centered, axis=-1, keepdims=True) + 1e-06)
    return centered * inverse, inverse


def norm_backward_pass(grad_hat, normal, inverse):
    first = jnp.mean(grad_hat, axis=-1, keepdims=True)
    second = jnp.mean(grad_hat * normal, axis=-1, keepdims=True)
    return (grad_hat - first - normal * second) * inverse


def dot(a, b, ca, cb):
    return lax.dot_general(a, b, (((ca,), (cb,)), ((), ())), preferred_element_type=F32)


def hi_lo(value):
    hi = value.astype(BF)
    lo = (value - hi.astype(F32)).astype(BF)
    return hi, lo


def pack(sums):
    hi = sums.astype(BF).astype(F32)
    row = lax.broadcasted_iota(jnp.int32, sums.shape, 0)
    return jnp.where(row % 4 < 2, hi, sums - hi).astype(BF)


def head_kernel(
    core_ref, x_ref, own_ref, other_ref, grad_ref, q_gain_ref, k_gain_ref,
    context_ref, dqkv_ref, part_ref, gains_ref, full_ref,
):
    rows, hd = grad_ref.shape
    lane = rows // 2
    blocks, w_rows, columns = own_ref.shape
    share = w_rows // 2
    own_first = core_ref[0] == 0
    for at in range(blocks):
        own, other = own_ref[at], other_ref[at]
        full_ref[2 * at] = jnp.where(own_first, own, other)
        full_ref[2 * at + 1] = jnp.where(own_first, other, own)
    full = full_ref[...].reshape(2 * blocks * w_rows, columns)
    product = dot(x_ref[...], full, 1, 0)
    raw = product[:rows]
    weighted = product[rows : rows + 1] + product[rows + 1 : rows + 2]

    q_gain, k_gain, grad = q_gain_ref[...], k_gain_ref[...], grad_ref[...]
    scale = hd ** (-0.5)
    qhat, q_inv = head_norm(raw[:, :hd])
    khat, k_inv = head_norm(raw[:, hd : 2 * hd])
    value = raw[:, 2 * hd :].astype(BF)
    q_norm = (qhat * q_gain).astype(BF)
    k_norm = (khat * k_gain).astype(BF)
    expo = jnp.exp(dot(q_norm, k_norm, 1, 1) * scale)
    probs = expo / jnp.sum(expo, axis=-1, keepdims=True)
    probs_b = probs.astype(BF)
    context_ref[...] = dot(probs_b, value, 1, 0).astype(BF)
    dprob = dot(grad, value, 1, 1)
    dscore = (probs * (dprob - jnp.sum(probs * dprob, axis=-1, keepdims=True)) * scale).astype(BF)
    dqn = dot(dscore, k_norm, 1, 0)
    dkn = dot(dscore, q_norm, 0, 0)
    gains_ref[0:1] = jnp.sum(dqn * qhat, axis=0, keepdims=True)
    gains_ref[1:2] = jnp.sum(dkn * khat, axis=0, keepdims=True)
    gains_ref[2:] = jnp.zeros((gains_ref.shape[0] - 2, hd), F32)
    dqkv = jnp.concatenate(
        [
            norm_backward_pass(dqn * q_gain, qhat, q_inv).astype(BF),
            norm_backward_pass(dkn * k_gain, khat, k_inv).astype(BF),
            dot(probs_b, grad, 0, 0).astype(BF),
        ],
        axis=1,
    )
    dqkv_ref[...] = dqkv

    for k in range(blocks):
        pair = full_ref[2 * k : 2 * k + 2].reshape(2 * w_rows, columns)
        part = dot(pair, dqkv, 1, 1).astype(BF)
        for group in range(4):
            for half in range(2):
                at = (2 * k + half) * share
                part_ref[group, at : at + share] = part[
                    group * share : (group + 1) * share, half * lane : (half + 1) * lane
                ]

    row = lax.broadcasted_iota(jnp.int32, (8, columns), 0)
    w_hi, w_lo = hi_lo(jnp.where(row % 2 == 0, weighted, 0.0))
    ones = jnp.where(row % 2 == 1, 1.0, 0.0).astype(BF)
    p_hi, p_lo = hi_lo(dqkv.astype(F32) * raw)
    sums = (dot(w_hi, dqkv, 1, 1) + dot(w_lo, dqkv, 1, 1)) + (
        dot(ones, p_hi, 1, 1) + dot(ones, p_lo, 1, 1)
    )
    packed = pack(jnp.concatenate([sums[:, :lane], sums[:, lane:]], axis=0))
    for group in range(4):
        part_ref[group, 2 * blocks * share :] = packed


def run_head(core, x, own, other, grad, q_gain, k_gain):
    rows, hd = grad.shape
    blocks, w_rows, columns = own.shape
    vmem = pl.BlockSpec(memory_space=pltpu.VMEM)
    return pl.pallas_call(
        head_kernel,
        in_specs=[pl.BlockSpec(memory_space=pltpu.SMEM)] + [vmem] * 6,
        out_specs=[vmem] * 4,
        out_shape=[
            jax.ShapeDtypeStruct((rows, hd), BF),
            jax.ShapeDtypeStruct((rows, columns), BF),
            jax.ShapeDtypeStruct((4, blocks * w_rows + 16, rows // 2), BF),
            jax.ShapeDtypeStruct((8, hd), F32),
        ],
        scratch_shapes=[pltpu.VMEM((2 * blocks, w_rows, columns), BF)],
        compiler_params=pltpu.CompilerParams(vmem_limit_bytes=20 * 2**20),
        cost_estimate=pl.CostEstimate(
            flops=1_400_000_000, bytes_accessed=9_000_000, transcendentals=65536
        ),
    )(core.reshape(1), x, own, other, grad, q_gain, k_gain)


def term_of(x_ref, dqkv, at, w_rows):
    columns = pl.ds(pl.multiple_of(2 * w_rows * at, 128), 2 * w_rows)
    term = dot(x_ref[:, columns], dqkv, 0, 0)
    return term[:w_rows], term[w_rows:]


def send_kernel(core_ref, x_ref, dqkv_ref, send_ref):
    dqkv = dqkv_ref[...]
    for at in range(send_ref.shape[0]):
        zero, one = term_of(x_ref, dqkv, at, send_ref.shape[1])
        send_ref[at] = jnp.where(core_ref[0] == 0, one, zero).astype(BF)


def chip_kernel(core_ref, x_at_ref, x_ref, dqkv_ref, got_ref, *out_refs):
    dqkv = dqkv_ref[...]
    for step, out_ref in enumerate(out_refs):
        first = lax.rem(x_at_ref[0] + step, NX) * NYL
        for y in range(NYL):
            zero, one = term_of(x_ref, dqkv, first + y, out_ref.shape[1])
            own = jnp.where(core_ref[0] == 0, zero, one)
            out_ref[y] = (own + got_ref[first + y].astype(F32)).astype(BF)


def w_grad_send(core, x, dqkv, shape):
    vmem, smem = (pl.BlockSpec(memory_space=space) for space in (pltpu.VMEM, pltpu.SMEM))
    return pl.pallas_call(
        send_kernel,
        in_specs=[smem, vmem, vmem],
        out_specs=vmem,
        out_shape=jax.ShapeDtypeStruct(shape, BF),
        compiler_params=pltpu.CompilerParams(vmem_limit_bytes=12 * 2**20),
    )(core.reshape(1), x, dqkv)


def chip_sum(core, x_at, x, dqkv, got):
    vmem, smem = (pl.BlockSpec(memory_space=space) for space in (pltpu.VMEM, pltpu.SMEM))
    return pl.pallas_call(
        chip_kernel,
        in_specs=[smem, smem, vmem, vmem, vmem],
        out_specs=[vmem] * NX,
        out_shape=[jax.ShapeDtypeStruct((NYL,) + got.shape[1:], BF)] * NX,
        compiler_params=pltpu.CompilerParams(vmem_limit_bytes=12 * 2**20),
    )(core.reshape(1), x_at.reshape(1), x, dqkv, got)


def near_kernel(near_ref, *refs):
    out_ref = refs[-1]
    blocks, chunk = out_ref.shape[0], out_ref.shape[1] - 16
    add = lambda at, size: sum(
        near_ref[group, at : at + size].astype(F32) for group in range(near_ref.shape[0])
    )
    got = add(blocks * chunk, 16)
    row = lax.broadcasted_iota(jnp.int32, got.shape, 0)
    both = got + pltpu.roll(got, 14, 0)
    packed = pack(jnp.where(row % 8 < 2, both, pltpu.roll(both, 2, 0)))
    for k in range(blocks):
        out_ref[k, :chunk] = add(k * chunk, chunk).astype(BF)
        out_ref[k, chunk:] = packed


def sum_near(near, order):
    vmem = pl.BlockSpec(memory_space=pltpu.VMEM)
    blocks = NZ // 2
    chunk = (near.shape[1] - 16) // blocks
    return pl.pallas_call(
        near_kernel,
        in_specs=[vmem] + [pl.BlockSpec(memory_space=pl.ANY)] * len(order),
        out_specs=vmem,
        out_shape=jax.ShapeDtypeStruct((blocks, chunk + 16, near.shape[2]), BF),
        compiler_params=pltpu.CompilerParams(vmem_limit_bytes=8 * 2**20),
    )(near, *order)


def far_kernel(width, far_ref, xhat_ref, gain_ref, inverse_ref, heads_ref, rows_ref, small_ref):
    share = xhat_ref.shape[0]
    lane = far_ref.shape[2]
    total = sum(far_ref[k].astype(F32) for k in range(far_ref.shape[0]))
    last = 2 * share
    product = jnp.zeros((share, lane), F32)
    for half in range(2):
        at = slice(half * lane, (half + 1) * lane)
        dnormed = total[half * share : (half + 1) * share]
        sums = total[last + 8 * half : last + 8 * half + 8]
        plain = sums[0:1] + sums[2:3]
        cross = sums[1:2] + sums[3:4]
        xhat = xhat_ref[:, at]
        rows_ref[:, at] = (
            (dnormed * gain_ref[...] - plain / width - xhat * (cross / width))
            * inverse_ref[:, at]
        ).astype(BF)
        product = product + dnormed * xhat
    small_ref[0] = heads_ref[...]
    small_ref[0, 7:8, :share] = jnp.sum(product.T, axis=0, keepdims=True)
    small = small_ref[0]
    for at in range(1, small_ref.shape[0]):
        small_ref[at] = small


def finish(width, far, xhat, gain, inverse, head_gains):
    vmem = pl.BlockSpec(memory_space=pltpu.VMEM)
    return pl.pallas_call(
        functools.partial(far_kernel, width),
        in_specs=[vmem] * 5,
        out_specs=[vmem] * 2,
        out_shape=[
            jax.ShapeDtypeStruct(xhat.shape, BF),
            jax.ShapeDtypeStruct((NX * NYL * NC,) + head_gains.shape, F32),
        ],
        compiler_params=pltpu.CompilerParams(vmem_limit_bytes=8 * 2**20),
    )(far, xhat, gain, inverse, head_gains)


def per_device(tokens, layer_norm_gain, w_qkv, q_gain, k_gain, ctx_grad):
    rows, width = tokens.shape
    w_rows, columns = w_qkv.shape
    share = width // (NZ * NYH)
    core = lax.axis_index(DP) % 2
    y_lo = (lax.axis_index(DP) // NC) % NYL
    x_at = lax.axis_index(DP) // (NYL * NC)
    mp = lax.axis_index(MP)
    lane = rows // 2

    with jax.named_scope("gather_w"):
        copies = jnp.broadcast_to(w_qkv[None], (NX * NYL, w_rows, columns))
        own = lax.all_to_all(copies, DP, 0, 0, axis_index_groups=SAME_CORE, tiled=True)
        other = lax.ppermute(own, DP, CORE_SWAP)

    with jax.named_scope("input_norm"):
        x_float = tokens.astype(F32)
        mean = jnp.mean(x_float, axis=-1, keepdims=True)
        centered = x_float - mean
        inverse = lax.rsqrt(jnp.mean(centered * centered, axis=-1, keepdims=True) + 1e-06)
        normed = (centered * inverse * layer_norm_gain).astype(BF)

        extra = jnp.concatenate(
            [jnp.stack(hi_lo(layer_norm_gain)), jnp.zeros((14, width), BF)], axis=0
        )
        lhs = jnp.concatenate([normed, extra], axis=0)

    with jax.named_scope("head"):
        context, dqkv, part, head_gains = run_head(
            core, lhs, own, other, ctx_grad, q_gain, k_gain
        )

    with jax.named_scope("input_gradient_near"):
        near = lax.all_to_all(part, MP, 0, 0, axis_index_groups=NEAR, tiled=True)

    with jax.named_scope("w_grad"):
        send = w_grad_send(core, normed, dqkv, (NX * NYL, w_rows, columns))
        got = lax.ppermute(send, DP, CORE_SWAP)
        x_term, *leaves = chip_sum(core, x_at, normed, dqkv, got)
        x_got = [lax.ppermute(leaf, DP, pairs) for leaf, pairs in zip(leaves, X_STEPS)]

    with jax.named_scope("sum_over_near"):
        pair = sum_near(near, [x_got[0], x_got[2]])
        far = lax.all_to_all(pair, MP, 0, 0, axis_index_groups=FAR, tiled=True)

    with jax.named_scope("w_grad_y"):
        x_term = sum(got.astype(F32) for got in [x_term, *x_got])
        leaves = jnp.where(y_lo == 0, x_term[1], x_term[0]).astype(BF)
        stays = jnp.where(y_lo == 0, x_term[0], x_term[1])
        w_grad = (stays + lax.ppermute(leaves, DP, YLO_SWAP).astype(F32)).astype(BF)

    with jax.named_scope("input_gradient"):
        start = mp * share
        tokens_share = lax.dynamic_slice_in_dim(tokens, start, share, 1).astype(F32)
        xhat_share = ((tokens_share - mean) * inverse).T
        gain_share = lax.dynamic_slice_in_dim(layer_norm_gain, start, share, 0)
        gradient, copies = finish(
            width, far, xhat_share, gain_share[:, None], inverse.T, head_gains
        )

    with jax.named_scope("gain_gradients"):
        summed = jnp.sum(lax.all_to_all(copies, DP, 0, 0, tiled=True), axis=0)
    return (
        context,
        gradient.T,
        summed[7, :share],
        w_grad,
        summed[0:1],
        summed[1:2],
    )


def solution(mesh):
    placed = (P("dp", None), P(), P("dp", "mp"), P("mp", None), P("mp", None), P("dp", "mp"))
    return jax.shard_map(
        per_device,
        mesh=mesh,
        in_specs=placed,
        out_specs=(
            P("dp", "mp"),
            P("dp", "mp"),
            P("mp"),
            P("dp", "mp"),
            P("mp", None),
            P("mp", None),
        ),
        check_vma=False,
    )
```

```python
import functools

import jax
import jax.numpy as jnp
from jax import lax
from jax.experimental import pallas as pl
from jax.experimental.pallas import tpu as pltpu
from jax.sharding import PartitionSpec as P

BF = jnp.bfloat16
F32 = jnp.float32
PATCHES = 256
DP, MP = "dp", "mp"
NX, NYL, NC = 4, 2, 2
NZ, NYH = 16, 2

CORE_SWAP = [(i, i ^ 1) for i in range(NX * NYL * NC)]
SAME_CORE = [[2 * i + c for i in range(NX * NYL)] for c in range(NC)]
YLO_SWAP = [(i, i ^ 2) for i in range(NX * NYL * NC)]
X_STEPS = [
    [(i, (i + step * NYL * NC) % (NX * NYL * NC)) for i in range(NX * NYL * NC)]
    for step in range(1, NX)
]
NEAR = [[2 * z + j for j in range(2 * NYH)] for z in range(0, NZ, 2)]
FAR = [[2 * NYH * k + j for k in range(NZ // 2)] for j in range(2 * NYH)]


def head_norm(raw):
    centered = raw - jnp.mean(raw, axis=-1, keepdims=True)
    inverse = lax.rsqrt(jnp.mean(centered * centered, axis=-1, keepdims=True) + 1e-06)
    return centered * inverse, inverse


def norm_backward_pass(grad_hat, normal, inverse):
    first = jnp.mean(grad_hat, axis=-1, keepdims=True)
    second = jnp.mean(grad_hat * normal, axis=-1, keepdims=True)
    return (grad_hat - first - normal * second) * inverse


def dot(a, b, ca, cb):
    return lax.dot_general(a, b, (((ca,), (cb,)), ((), ())), preferred_element_type=F32)


def hi_lo(value):
    hi = value.astype(BF)
    lo = (value - hi.astype(F32)).astype(BF)
    return hi, lo


def pack(sums):
    hi = sums.astype(BF).astype(F32)
    row = lax.broadcasted_iota(jnp.int32, sums.shape, 0)
    return jnp.where(row % 4 < 2, hi, sums - hi).astype(BF)


def head_kernel(
    core_ref, x_ref, own_ref, other_ref, grad_ref, q_gain_ref, k_gain_ref,
    context_ref, dqkv_ref, part_ref, gains_ref, full_ref,
):
    rows, hd = grad_ref.shape
    lane = rows // 2
    blocks, w_rows, columns = own_ref.shape
    share = w_rows // 2
    own_first = core_ref[0] == 0
    for at in range(blocks):
        own, other = own_ref[at], other_ref[at]
        full_ref[2 * at] = jnp.where(own_first, own, other)
        full_ref[2 * at + 1] = jnp.where(own_first, other, own)
    full = full_ref[...].reshape(2 * blocks * w_rows, columns)
    product = dot(x_ref[...], full, 1, 0)
    raw = product[:rows]
    weighted = product[rows : rows + 1] + product[rows + 1 : rows + 2]

    q_gain, k_gain, grad = q_gain_ref[...], k_gain_ref[...], grad_ref[...]
    scale = hd ** (-0.5)
    qhat, q_inv = head_norm(raw[:, :hd])
    khat, k_inv = head_norm(raw[:, hd : 2 * hd])
    value = raw[:, 2 * hd :].astype(BF)
    q_norm = (qhat * q_gain).astype(BF)
    k_norm = (khat * k_gain).astype(BF)
    expo = jnp.exp(dot(q_norm, k_norm, 1, 1) * scale)
    probs = expo / jnp.sum(expo, axis=-1, keepdims=True)
    probs_b = probs.astype(BF)
    context_ref[...] = dot(probs_b, value, 1, 0).astype(BF)
    dprob = dot(grad, value, 1, 1)
    dscore = (probs * (dprob - jnp.sum(probs * dprob, axis=-1, keepdims=True)) * scale).astype(BF)
    dqn = dot(dscore, k_norm, 1, 0)
    dkn = dot(dscore, q_norm, 0, 0)
    gains_ref[0:1] = jnp.sum(dqn * qhat, axis=0, keepdims=True)
    gains_ref[1:2] = jnp.sum(dkn * khat, axis=0, keepdims=True)
    gains_ref[2:] = jnp.zeros((gains_ref.shape[0] - 2, hd), F32)
    dqkv = jnp.concatenate(
        [
            norm_backward_pass(dqn * q_gain, qhat, q_inv).astype(BF),
            norm_backward_pass(dkn * k_gain, khat, k_inv).astype(BF),
            dot(probs_b, grad, 0, 0).astype(BF),
        ],
        axis=1,
    )
    dqkv_ref[...] = dqkv

    for k in range(blocks):
        pair = full_ref[2 * k : 2 * k + 2].reshape(2 * w_rows, columns)
        part = dot(pair, dqkv, 1, 1).astype(BF)
        for group in range(4):
            for half in range(2):
                at = (2 * k + half) * share
                part_ref[group, at : at + share] = part[
                    group * share : (group + 1) * share, half * lane : (half + 1) * lane
                ]

    row = lax.broadcasted_iota(jnp.int32, (8, columns), 0)
    w_hi, w_lo = hi_lo(jnp.where(row % 2 == 0, weighted, 0.0))
    ones = jnp.where(row % 2 == 1, 1.0, 0.0).astype(BF)
    p_hi, p_lo = hi_lo(dqkv.astype(F32) * raw)
    sums = (dot(w_hi, dqkv, 1, 1) + dot(w_lo, dqkv, 1, 1)) + (
        dot(ones, p_hi, 1, 1) + dot(ones, p_lo, 1, 1)
    )
    packed = pack(jnp.concatenate([sums[:, :lane], sums[:, lane:]], axis=0))
    for group in range(4):
        part_ref[group, 2 * blocks * share :] = packed


def run_head(core, x, own, other, grad, q_gain, k_gain):
    rows, hd = grad.shape
    blocks, w_rows, columns = own.shape
    vmem = pl.BlockSpec(memory_space=pltpu.VMEM)
    return pl.pallas_call(
        head_kernel,
        in_specs=[pl.BlockSpec(memory_space=pltpu.SMEM)] + [vmem] * 6,
        out_specs=[vmem] * 4,
        out_shape=[
            jax.ShapeDtypeStruct((rows, hd), BF),
            jax.ShapeDtypeStruct((rows, columns), BF),
            jax.ShapeDtypeStruct((4, blocks * w_rows + 16, rows // 2), BF),
            jax.ShapeDtypeStruct((8, hd), F32),
        ],
        scratch_shapes=[pltpu.VMEM((2 * blocks, w_rows, columns), BF)],
        compiler_params=pltpu.CompilerParams(vmem_limit_bytes=48 * 2**20),
        cost_estimate=pl.CostEstimate(
            flops=1_400_000_000, bytes_accessed=9_000_000, transcendentals=65536
        ),
    )(core.reshape(1), x, own, other, grad, q_gain, k_gain)


def near_kernel(near_ref, *refs):
    out_ref = refs[-1]
    blocks, chunk = out_ref.shape[0], out_ref.shape[1] - 16
    add = lambda at, size: sum(
        near_ref[group, at : at + size].astype(F32) for group in range(near_ref.shape[0])
    )
    got = add(blocks * chunk, 16)
    row = lax.broadcasted_iota(jnp.int32, got.shape, 0)
    both = got + pltpu.roll(got, 14, 0)
    packed = pack(jnp.where(row % 8 < 2, both, pltpu.roll(both, 2, 0)))
    for k in range(blocks):
        out_ref[k, :chunk] = add(k * chunk, chunk).astype(BF)
        out_ref[k, chunk:] = packed


def sum_near(near, order):
    vmem = pl.BlockSpec(memory_space=pltpu.VMEM)
    blocks = NZ // 2
    chunk = (near.shape[1] - 16) // blocks
    return pl.pallas_call(
        near_kernel,
        in_specs=[vmem] + [pl.BlockSpec(memory_space=pl.ANY)] * len(order),
        out_specs=vmem,
        out_shape=jax.ShapeDtypeStruct((blocks, chunk + 16, near.shape[2]), BF),
        compiler_params=pltpu.CompilerParams(vmem_limit_bytes=24 * 2**20),
    )(near, *order)


def far_kernel(width, far_ref, xhat_ref, gain_ref, inverse_ref, heads_ref, rows_ref, small_ref):
    share = xhat_ref.shape[0]
    lane = far_ref.shape[2]
    total = sum(far_ref[k].astype(F32) for k in range(far_ref.shape[0]))
    last = 2 * share
    product = jnp.zeros((share, lane), F32)
    for half in range(2):
        at = slice(half * lane, (half + 1) * lane)
        dnormed = total[half * share : (half + 1) * share]
        sums = total[last + 8 * half : last + 8 * half + 8]
        plain = sums[0:1] + sums[2:3]
        cross = sums[1:2] + sums[3:4]
        xhat = xhat_ref[:, at]
        rows_ref[:, at] = (
            (dnormed * gain_ref[...] - plain / width - xhat * (cross / width))
            * inverse_ref[:, at]
        ).astype(BF)
        product = product + dnormed * xhat
    small_ref[0] = heads_ref[...]
    small_ref[0, 7:8, :share] = jnp.sum(product.T, axis=0, keepdims=True)
    small = small_ref[0]
    for at in range(1, small_ref.shape[0]):
        small_ref[at] = small


def finish(width, far, xhat, gain, inverse, head_gains):
    vmem = pl.BlockSpec(memory_space=pltpu.VMEM)
    return pl.pallas_call(
        functools.partial(far_kernel, width),
        in_specs=[vmem] * 5,
        out_specs=[vmem] * 2,
        out_shape=[
            jax.ShapeDtypeStruct(xhat.shape, BF),
            jax.ShapeDtypeStruct((NX * NYL * NC,) + head_gains.shape, F32),
        ],
        compiler_params=pltpu.CompilerParams(vmem_limit_bytes=24 * 2**20),
    )(far, xhat, gain, inverse, head_gains)


def per_device(tokens, layer_norm_gain, w_qkv, q_gain, k_gain, ctx_grad):
    rows, width = tokens.shape
    w_rows, columns = w_qkv.shape
    share = width // (NZ * NYH)
    core = lax.axis_index(DP) % 2
    y_lo = (lax.axis_index(DP) // NC) % NYL
    x_at = lax.axis_index(DP) // (NYL * NC)
    mp = lax.axis_index(MP)
    lane = rows // 2

    with jax.named_scope("gather_w"):
        copies = jnp.broadcast_to(w_qkv[None], (NX * NYL, w_rows, columns))
        own = lax.all_to_all(copies, DP, 0, 0, axis_index_groups=SAME_CORE, tiled=True)
        other = lax.ppermute(own, DP, CORE_SWAP)

    with jax.named_scope("input_norm"):
        x_float = tokens.astype(F32)
        mean = jnp.mean(x_float, axis=-1, keepdims=True)
        centered = x_float - mean
        inverse = lax.rsqrt(jnp.mean(centered * centered, axis=-1, keepdims=True) + 1e-06)
        normed = (centered * inverse * layer_norm_gain).astype(BF)

        extra = jnp.concatenate(
            [jnp.stack(hi_lo(layer_norm_gain)), jnp.zeros((14, width), BF)], axis=0
        )
        lhs = jnp.concatenate([normed, extra], axis=0)

    with jax.named_scope("head"):
        context, dqkv, part, head_gains = run_head(
            core, lhs, own, other, ctx_grad, q_gain, k_gain
        )

    with jax.named_scope("input_gradient_near"):
        near = lax.all_to_all(part, MP, 0, 0, axis_index_groups=NEAR, tiled=True)

    with jax.named_scope("w_grad"):
        term = dot(normed, dqkv, 0, 0).astype(BF).reshape(NX * NYL, NC, w_rows, columns)
        term_keep = jnp.where(core == 0, term[:, 0], term[:, 1])
        term_send = jnp.where(core == 0, term[:, 1], term[:, 0])
        term_got = lax.ppermute(term_send, DP, CORE_SWAP)
        chip = (term_keep.astype(F32) + term_got.astype(F32)).astype(BF)
        chip = chip.reshape(NX, NYL, w_rows, columns)
        x_term = lax.dynamic_index_in_dim(chip, x_at, 0, False).astype(F32)
        x_got = [
            lax.ppermute(
                lax.dynamic_index_in_dim(chip, (x_at + step) % NX, 0, False), DP, pairs
            )
            for step, pairs in enumerate(X_STEPS, 1)
        ]

    with jax.named_scope("sum_over_near"):
        pair = sum_near(near, [x_got[0]])
        far = lax.all_to_all(pair, MP, 0, 0, axis_index_groups=FAR, tiled=True)

    with jax.named_scope("w_grad_y"):
        x_term = x_term + sum(got.astype(F32) for got in x_got)
        leaves = jnp.where(y_lo == 0, x_term[1], x_term[0]).astype(BF)
        stays = jnp.where(y_lo == 0, x_term[0], x_term[1])
        w_grad = (stays + lax.ppermute(leaves, DP, YLO_SWAP).astype(F32)).astype(BF)

    with jax.named_scope("input_gradient"):
        start = mp * share
        tokens_share = lax.dynamic_slice_in_dim(tokens, start, share, 1).astype(F32)
        xhat_share = ((tokens_share - mean) * inverse).T
        gain_share = lax.dynamic_slice_in_dim(layer_norm_gain, start, share, 0)
        gradient, copies = finish(
            width, far, xhat_share, gain_share[:, None], inverse.T, head_gains
        )

    with jax.named_scope("gain_gradients"):
        summed = jnp.sum(lax.all_to_all(copies, DP, 0, 0, tiled=True), axis=0)
    return (
        context,
        gradient.T,
        summed[7, :share],
        w_grad,
        summed[0:1],
        summed[1:2],
    )


def solution(mesh):
    placed = (P("dp", None), P(), P("dp", "mp"), P("mp", None), P("mp", None), P("dp", "mp"))
    return jax.shard_map(
        per_device,
        mesh=mesh,
        in_specs=placed,
        out_specs=(
            P("dp", "mp"),
            P("dp", "mp"),
            P("mp"),
            P("dp", "mp"),
            P("mp", None),
            P("mp", None),
        ),
        check_vma=False,
    )
```

```python
import functools

import jax
import jax.numpy as jnp
from jax import lax
from jax.experimental import pallas as pl
from jax.experimental.pallas import tpu as pltpu
from jax.sharding import PartitionSpec as P

BF = jnp.bfloat16
F32 = jnp.float32
PATCHES = 256
DP, MP = "dp", "mp"
NX, NYL, NC = 4, 2, 2
NZ, NYH = 16, 2

CORE_SWAP = [(i, i ^ 1) for i in range(NX * NYL * NC)]
SAME_CORE = [[2 * i + c for i in range(NX * NYL)] for c in range(NC)]
YLO_SWAP = [(i, i ^ 2) for i in range(NX * NYL * NC)]
X_STEPS = [
    [(i, (i + step * NYL * NC) % (NX * NYL * NC)) for i in range(NX * NYL * NC)]
    for step in range(1, NX)
]
NEAR = [[2 * z + j for j in range(2 * NYH)] for z in range(0, NZ, 2)]
FAR = [[2 * NYH * k + j for k in range(NZ // 2)] for j in range(2 * NYH)]


def head_norm(raw):
    centered = raw - jnp.mean(raw, axis=-1, keepdims=True)
    inverse = lax.rsqrt(jnp.mean(centered * centered, axis=-1, keepdims=True) + 1e-06)
    return centered * inverse, inverse


def norm_backward_pass(grad_hat, normal, inverse):
    first = jnp.mean(grad_hat, axis=-1, keepdims=True)
    second = jnp.mean(grad_hat * normal, axis=-1, keepdims=True)
    return (grad_hat - first - normal * second) * inverse


def dot(a, b, ca, cb):
    return lax.dot_general(a, b, (((ca,), (cb,)), ((), ())), preferred_element_type=F32)


def hi_lo(value):
    hi = value.astype(BF)
    lo = (value - hi.astype(F32)).astype(BF)
    return hi, lo


def pack(sums):
    hi = sums.astype(BF).astype(F32)
    row = lax.broadcasted_iota(jnp.int32, sums.shape, 0)
    return jnp.where(row % 4 < 2, hi, sums - hi).astype(BF)


def head_kernel(
    core_ref, x_ref, own_ref, other_ref, grad_ref, q_gain_ref, k_gain_ref,
    context_ref, dqkv_ref, part_ref, gains_ref, full_ref,
):
    rows, hd = grad_ref.shape
    lane = rows // 2
    blocks, w_rows, columns = own_ref.shape
    share = w_rows // 2
    own_first = core_ref[0] == 0
    for at in range(blocks):
        own, other = own_ref[at], other_ref[at]
        full_ref[2 * at] = jnp.where(own_first, own, other)
        full_ref[2 * at + 1] = jnp.where(own_first, other, own)
    full = full_ref[...].reshape(2 * blocks * w_rows, columns)
    product = dot(x_ref[...], full, 1, 0)
    raw = product[:rows]
    weighted = product[rows : rows + 1] + product[rows + 1 : rows + 2]

    q_gain, k_gain, grad = q_gain_ref[...], k_gain_ref[...], grad_ref[...]
    scale = hd ** (-0.5)
    qhat, q_inv = head_norm(raw[:, :hd])
    khat, k_inv = head_norm(raw[:, hd : 2 * hd])
    value = raw[:, 2 * hd :].astype(BF)
    q_norm = (qhat * q_gain).astype(BF)
    k_norm = (khat * k_gain).astype(BF)
    expo = jnp.exp(dot(q_norm, k_norm, 1, 1) * scale)
    probs = expo / jnp.sum(expo, axis=-1, keepdims=True)
    probs_b = probs.astype(BF)
    context_ref[...] = dot(probs_b, value, 1, 0).astype(BF)
    dprob = dot(grad, value, 1, 1)
    dscore = (probs * (dprob - jnp.sum(probs * dprob, axis=-1, keepdims=True)) * scale).astype(BF)
    dqn = dot(dscore, k_norm, 1, 0)
    dkn = dot(dscore, q_norm, 0, 0)
    gains_ref[0:1] = jnp.sum(dqn * qhat, axis=0, keepdims=True)
    gains_ref[1:2] = jnp.sum(dkn * khat, axis=0, keepdims=True)
    gains_ref[2:] = jnp.zeros((gains_ref.shape[0] - 2, hd), F32)
    dqkv = jnp.concatenate(
        [
            norm_backward_pass(dqn * q_gain, qhat, q_inv).astype(BF),
            norm_backward_pass(dkn * k_gain, khat, k_inv).astype(BF),
            dot(probs_b, grad, 0, 0).astype(BF),
        ],
        axis=1,
    )
    dqkv_ref[...] = dqkv

    for k in range(blocks):
        pair = full_ref[2 * k : 2 * k + 2].reshape(2 * w_rows, columns)
        part = dot(pair, dqkv, 1, 1).astype(BF)
        for group in range(4):
            for half in range(2):
                at = (2 * k + half) * share
                part_ref[group, at : at + share] = part[
                    group * share : (group + 1) * share, half * lane : (half + 1) * lane
                ]

    row = lax.broadcasted_iota(jnp.int32, (8, columns), 0)
    w_hi, w_lo = hi_lo(jnp.where(row % 2 == 0, weighted, 0.0))
    ones = jnp.where(row % 2 == 1, 1.0, 0.0).astype(BF)
    p_hi, p_lo = hi_lo(dqkv.astype(F32) * raw)
    sums = (dot(w_hi, dqkv, 1, 1) + dot(w_lo, dqkv, 1, 1)) + (
        dot(ones, p_hi, 1, 1) + dot(ones, p_lo, 1, 1)
    )
    packed = pack(jnp.concatenate([sums[:, :lane], sums[:, lane:]], axis=0))
    for group in range(4):
        part_ref[group, 2 * blocks * share :] = packed


def run_head(core, x, own, other, grad, q_gain, k_gain):
    rows, hd = grad.shape
    blocks, w_rows, columns = own.shape
    vmem = pl.BlockSpec(memory_space=pltpu.VMEM)
    return pl.pallas_call(
        head_kernel,
        in_specs=[pl.BlockSpec(memory_space=pltpu.SMEM)] + [vmem] * 6,
        out_specs=[vmem] * 4,
        out_shape=[
            jax.ShapeDtypeStruct((rows, hd), BF),
            jax.ShapeDtypeStruct((rows, columns), BF),
            jax.ShapeDtypeStruct((4, blocks * w_rows + 16, rows // 2), BF),
            jax.ShapeDtypeStruct((8, hd), F32),
        ],
        scratch_shapes=[pltpu.VMEM((2 * blocks, w_rows, columns), BF)],
        compiler_params=pltpu.CompilerParams(vmem_limit_bytes=48 * 2**20),
        cost_estimate=pl.CostEstimate(
            flops=1_400_000_000, bytes_accessed=9_000_000, transcendentals=65536
        ),
    )(core.reshape(1), x, own, other, grad, q_gain, k_gain)


def near_kernel(near_ref, *refs):
    out_ref = refs[-1]
    blocks, chunk = out_ref.shape[0], out_ref.shape[1] - 16
    add = lambda at, size: sum(
        near_ref[group, at : at + size].astype(F32) for group in range(near_ref.shape[0])
    )
    got = add(blocks * chunk, 16)
    row = lax.broadcasted_iota(jnp.int32, got.shape, 0)
    both = got + pltpu.roll(got, 14, 0)
    packed = pack(jnp.where(row % 8 < 2, both, pltpu.roll(both, 2, 0)))
    for k in range(blocks):
        out_ref[k, :chunk] = add(k * chunk, chunk).astype(BF)
        out_ref[k, chunk:] = packed


def sum_near(near, order):
    vmem = pl.BlockSpec(memory_space=pltpu.VMEM)
    blocks = NZ // 2
    chunk = (near.shape[1] - 16) // blocks
    return pl.pallas_call(
        near_kernel,
        in_specs=[vmem] + [pl.BlockSpec(memory_space=pl.ANY)] * len(order),
        out_specs=vmem,
        out_shape=jax.ShapeDtypeStruct((blocks, chunk + 16, near.shape[2]), BF),
        compiler_params=pltpu.CompilerParams(vmem_limit_bytes=24 * 2**20),
    )(near, *order)


def far_kernel(width, far_ref, xhat_ref, gain_ref, inverse_ref, heads_ref, rows_ref, small_ref):
    share = xhat_ref.shape[0]
    lane = far_ref.shape[2]
    total = sum(far_ref[k].astype(F32) for k in range(far_ref.shape[0]))
    last = 2 * share
    product = jnp.zeros((share, lane), F32)
    for half in range(2):
        at = slice(half * lane, (half + 1) * lane)
        dnormed = total[half * share : (half + 1) * share]
        sums = total[last + 8 * half : last + 8 * half + 8]
        plain = sums[0:1] + sums[2:3]
        cross = sums[1:2] + sums[3:4]
        xhat = xhat_ref[:, at]
        rows_ref[:, at] = (
            (dnormed * gain_ref[...] - plain / width - xhat * (cross / width))
            * inverse_ref[:, at]
        ).astype(BF)
        product = product + dnormed * xhat
    small_ref[0] = heads_ref[...]
    small_ref[0, 7:8, :share] = jnp.sum(product.T, axis=0, keepdims=True)
    small = small_ref[0]
    for at in range(1, small_ref.shape[0]):
        small_ref[at] = small


def finish(width, far, xhat, gain, inverse, head_gains):
    vmem = pl.BlockSpec(memory_space=pltpu.VMEM)
    return pl.pallas_call(
        functools.partial(far_kernel, width),
        in_specs=[vmem] * 5,
        out_specs=[vmem] * 2,
        out_shape=[
            jax.ShapeDtypeStruct(xhat.shape, BF),
            jax.ShapeDtypeStruct((NX * NYL * NC,) + head_gains.shape, F32),
        ],
        compiler_params=pltpu.CompilerParams(vmem_limit_bytes=24 * 2**20),
    )(far, xhat, gain, inverse, head_gains)


def per_device(tokens, layer_norm_gain, w_qkv, q_gain, k_gain, ctx_grad):
    rows, width = tokens.shape
    w_rows, columns = w_qkv.shape
    share = width // (NZ * NYH)
    core = lax.axis_index(DP) % 2
    y_lo = (lax.axis_index(DP) // NC) % NYL
    x_at = lax.axis_index(DP) // (NYL * NC)
    mp = lax.axis_index(MP)
    lane = rows // 2

    with jax.named_scope("gather_w"):
        copies = jnp.broadcast_to(w_qkv[None], (NX * NYL, w_rows, columns))
        own = lax.all_to_all(copies, DP, 0, 0, axis_index_groups=SAME_CORE, tiled=True)
        other = lax.ppermute(own, DP, CORE_SWAP)

    with jax.named_scope("input_norm"):
        x_float = tokens.astype(F32)
        mean = jnp.mean(x_float, axis=-1, keepdims=True)
        centered = x_float - mean
        inverse = lax.rsqrt(jnp.mean(centered * centered, axis=-1, keepdims=True) + 1e-06)
        normed = (centered * inverse * layer_norm_gain).astype(BF)

        extra = jnp.concatenate(
            [jnp.stack(hi_lo(layer_norm_gain)), jnp.zeros((14, width), BF)], axis=0
        )
        lhs = jnp.concatenate([normed, extra], axis=0)

    with jax.named_scope("head"):
        context, dqkv, part, head_gains = run_head(
            core, lhs, own, other, ctx_grad, q_gain, k_gain
        )

    with jax.named_scope("input_gradient_near"):
        near = lax.all_to_all(part, MP, 0, 0, axis_index_groups=NEAR, tiled=True)

    with jax.named_scope("w_grad"):
        term = dot(normed, dqkv, 0, 0).astype(BF).reshape(NX * NYL, NC, w_rows, columns)
        term_keep = jnp.where(core == 0, term[:, 0], term[:, 1])
        term_send = jnp.where(core == 0, term[:, 1], term[:, 0])
        term_got = lax.ppermute(term_send, DP, CORE_SWAP)
        chip = (term_keep.astype(F32) + term_got.astype(F32)).astype(BF)
        chip = chip.reshape(NX, NYL, w_rows, columns)
        x_term = lax.dynamic_index_in_dim(chip, x_at, 0, False).astype(F32)
        x_got = [
            lax.ppermute(
                lax.dynamic_index_in_dim(chip, (x_at + step) % NX, 0, False), DP, pairs
            )
            for step, pairs in enumerate(X_STEPS, 1)
        ]

    with jax.named_scope("sum_over_near"):
        pair = sum_near(near, [chip])
        far = lax.all_to_all(pair, MP, 0, 0, axis_index_groups=FAR, tiled=True)

    with jax.named_scope("w_grad_y"):
        x_term = x_term + sum(got.astype(F32) for got in x_got)
        leaves = jnp.where(y_lo == 0, x_term[1], x_term[0]).astype(BF)
        stays = jnp.where(y_lo == 0, x_term[0], x_term[1])
        w_grad = (stays + lax.ppermute(leaves, DP, YLO_SWAP).astype(F32)).astype(BF)

    with jax.named_scope("input_gradient"):
        start = mp * share
        tokens_share = lax.dynamic_slice_in_dim(tokens, start, share, 1).astype(F32)
        xhat_share = ((tokens_share - mean) * inverse).T
        gain_share = lax.dynamic_slice_in_dim(layer_norm_gain, start, share, 0)
        gradient, copies = finish(
            width, far, xhat_share, gain_share[:, None], inverse.T, head_gains
        )

    with jax.named_scope("gain_gradients"):
        summed = jnp.sum(lax.all_to_all(copies, DP, 0, 0, tiled=True), axis=0)
    return (
        context,
        gradient.T,
        summed[7, :share],
        w_grad,
        summed[0:1],
        summed[1:2],
    )


def solution(mesh):
    placed = (P("dp", None), P(), P("dp", "mp"), P("mp", None), P("mp", None), P("dp", "mp"))
    return jax.shard_map(
        per_device,
        mesh=mesh,
        in_specs=placed,
        out_specs=(
            P("dp", "mp"),
            P("dp", "mp"),
            P("mp"),
            P("dp", "mp"),
            P("mp", None),
            P("mp", None),
        ),
        check_vma=False,
    )
```

```python
import functools

import jax
import jax.numpy as jnp
from jax import lax
from jax.experimental import pallas as pl
from jax.experimental.pallas import tpu as pltpu
from jax.sharding import PartitionSpec as P

BF = jnp.bfloat16
F32 = jnp.float32
PATCHES = 256
DP, MP = "dp", "mp"
NX, NYL, NC = 4, 2, 2
NZ, NYH = 16, 2

CORE_SWAP = [(i, i ^ 1) for i in range(NX * NYL * NC)]
SAME_CORE = [[2 * i + c for i in range(NX * NYL)] for c in range(NC)]
YLO_SWAP = [(i, i ^ 2) for i in range(NX * NYL * NC)]
X_STEPS = [
    [(i, (i + step * NYL * NC) % (NX * NYL * NC)) for i in range(NX * NYL * NC)]
    for step in range(1, NX)
]
NEAR = [[2 * z + j for j in range(2 * NYH)] for z in range(0, NZ, 2)]
FAR = [[2 * NYH * k + j for k in range(NZ // 2)] for j in range(2 * NYH)]


def head_norm(raw):
    centered = raw - jnp.mean(raw, axis=-1, keepdims=True)
    inverse = lax.rsqrt(jnp.mean(centered * centered, axis=-1, keepdims=True) + 1e-06)
    return centered * inverse, inverse


def norm_backward_pass(grad_hat, normal, inverse):
    first = jnp.mean(grad_hat, axis=-1, keepdims=True)
    second = jnp.mean(grad_hat * normal, axis=-1, keepdims=True)
    return (grad_hat - first - normal * second) * inverse


def dot(a, b, ca, cb):
    return lax.dot_general(a, b, (((ca,), (cb,)), ((), ())), preferred_element_type=F32)


def hi_lo(value):
    hi = value.astype(BF)
    lo = (value - hi.astype(F32)).astype(BF)
    return hi, lo


def pack(sums):
    hi = sums.astype(BF).astype(F32)
    row = lax.broadcasted_iota(jnp.int32, sums.shape, 0)
    return jnp.where(row % 4 < 2, hi, sums - hi).astype(BF)


def head_kernel(
    core_ref, x_ref, own_ref, other_ref, grad_ref, q_gain_ref, k_gain_ref,
    context_ref, dqkv_ref, out_ref, gains_ref, full_ref, part_ref, sems,
):
    rows, hd = grad_ref.shape
    lane = rows // 2
    blocks, w_rows, columns = own_ref.shape
    share = w_rows // 2
    own_first = core_ref[0] == 0
    for at in range(blocks):
        own, other = own_ref[at], other_ref[at]
        full_ref[2 * at] = jnp.where(own_first, own, other)
        full_ref[2 * at + 1] = jnp.where(own_first, other, own)
    full = full_ref[...].reshape(2 * blocks * w_rows, columns)
    product = dot(x_ref[...], full, 1, 0)
    raw = product[:rows]
    weighted = product[rows : rows + 1] + product[rows + 1 : rows + 2]

    q_gain, k_gain, grad = q_gain_ref[...], k_gain_ref[...], grad_ref[...]
    scale = hd ** (-0.5)
    qhat, q_inv = head_norm(raw[:, :hd])
    khat, k_inv = head_norm(raw[:, hd : 2 * hd])
    value = raw[:, 2 * hd :].astype(BF)
    q_norm = (qhat * q_gain).astype(BF)
    k_norm = (khat * k_gain).astype(BF)
    expo = jnp.exp(dot(q_norm, k_norm, 1, 1) * scale)
    probs = expo / jnp.sum(expo, axis=-1, keepdims=True)
    probs_b = probs.astype(BF)
    context_ref[...] = dot(probs_b, value, 1, 0).astype(BF)
    dprob = dot(grad, value, 1, 1)
    dscore = (probs * (dprob - jnp.sum(probs * dprob, axis=-1, keepdims=True)) * scale).astype(BF)
    dqn = dot(dscore, k_norm, 1, 0)
    dkn = dot(dscore, q_norm, 0, 0)
    gains_ref[0:1] = jnp.sum(dqn * qhat, axis=0, keepdims=True)
    gains_ref[1:2] = jnp.sum(dkn * khat, axis=0, keepdims=True)
    gains_ref[2:] = jnp.zeros((gains_ref.shape[0] - 2, hd), F32)
    dqkv = jnp.concatenate(
        [
            norm_backward_pass(dqn * q_gain, qhat, q_inv).astype(BF),
            norm_backward_pass(dkn * k_gain, khat, k_inv).astype(BF),
            dot(probs_b, grad, 0, 0).astype(BF),
        ],
        axis=1,
    )
    dqkv_ref[...] = dqkv

    row = lax.broadcasted_iota(jnp.int32, (8, columns), 0)
    w_hi, w_lo = hi_lo(jnp.where(row % 2 == 0, weighted, 0.0))
    ones = jnp.where(row % 2 == 1, 1.0, 0.0).astype(BF)
    p_hi, p_lo = hi_lo(dqkv.astype(F32) * raw)
    sums = (dot(w_hi, dqkv, 1, 1) + dot(w_lo, dqkv, 1, 1)) + (
        dot(ones, p_hi, 1, 1) + dot(ones, p_lo, 1, 1)
    )
    packed = pack(jnp.concatenate([sums[:, :lane], sums[:, lane:]], axis=0))
    for group in range(4):
        part_ref[group, 2 * blocks * share :] = packed

    copies = []

    def leave(index, at, size):
        rows_at = pl.ds(at, size)
        copy = pltpu.make_async_copy(
            part_ref.at[:, rows_at], out_ref.at[:, rows_at], sems.at[index]
        )
        copy.start()
        copies.append(copy)

    leave(blocks, 2 * blocks * share, 16)

    for k in range(blocks):
        pair = full_ref[2 * k : 2 * k + 2].reshape(2 * w_rows, columns)
        part = dot(pair, dqkv, 1, 1).astype(BF)
        for group in range(4):
            for half in range(2):
                at = (2 * k + half) * share
                part_ref[group, at : at + share] = part[
                    group * share : (group + 1) * share, half * lane : (half + 1) * lane
                ]
        leave(k, 2 * k * share, 2 * share)
    for copy in copies:
        copy.wait()


def run_head(core, x, own, other, grad, q_gain, k_gain):
    rows, hd = grad.shape
    blocks, w_rows, columns = own.shape
    vmem = pl.BlockSpec(memory_space=pltpu.VMEM)
    return pl.pallas_call(
        head_kernel,
        in_specs=[pl.BlockSpec(memory_space=pltpu.SMEM)] + [vmem] * 6,
        out_specs=[vmem, vmem, pl.BlockSpec(memory_space=pl.ANY), vmem],
        out_shape=[
            jax.ShapeDtypeStruct((rows, hd), BF),
            jax.ShapeDtypeStruct((rows, columns), BF),
            jax.ShapeDtypeStruct((4, blocks * w_rows + 16, rows // 2), BF),
            jax.ShapeDtypeStruct((8, hd), F32),
        ],
        scratch_shapes=[
            pltpu.VMEM((2 * blocks, w_rows, columns), BF),
            pltpu.VMEM((4, blocks * w_rows + 16, rows // 2), BF),
            pltpu.SemaphoreType.DMA((blocks + 1,)),
        ],
        compiler_params=pltpu.CompilerParams(vmem_limit_bytes=48 * 2**20),
        cost_estimate=pl.CostEstimate(
            flops=1_400_000_000, bytes_accessed=9_000_000, transcendentals=65536
        ),
    )(core.reshape(1), x, own, other, grad, q_gain, k_gain)


def near_kernel(near_ref, *refs):
    out_ref = refs[-1]
    blocks, chunk = out_ref.shape[0], out_ref.shape[1] - 16
    add = lambda at, size: sum(
        near_ref[group, at : at + size].astype(F32) for group in range(near_ref.shape[0])
    )
    got = add(blocks * chunk, 16)
    row = lax.broadcasted_iota(jnp.int32, got.shape, 0)
    both = got + pltpu.roll(got, 14, 0)
    packed = pack(jnp.where(row % 8 < 2, both, pltpu.roll(both, 2, 0)))
    for k in range(blocks):
        out_ref[k, :chunk] = add(k * chunk, chunk).astype(BF)
        out_ref[k, chunk:] = packed


def sum_near(near, order):
    vmem = pl.BlockSpec(memory_space=pltpu.VMEM)
    blocks = NZ // 2
    chunk = (near.shape[1] - 16) // blocks
    return pl.pallas_call(
        near_kernel,
        in_specs=[vmem] + [pl.BlockSpec(memory_space=pl.ANY)] * len(order),
        out_specs=vmem,
        out_shape=jax.ShapeDtypeStruct((blocks, chunk + 16, near.shape[2]), BF),
        compiler_params=pltpu.CompilerParams(vmem_limit_bytes=24 * 2**20),
    )(near, *order)


def far_kernel(width, far_ref, xhat_ref, gain_ref, inverse_ref, heads_ref, rows_ref, small_ref):
    share = xhat_ref.shape[0]
    lane = far_ref.shape[2]
    total = sum(far_ref[k].astype(F32) for k in range(far_ref.shape[0]))
    last = 2 * share
    product = jnp.zeros((share, lane), F32)
    for half in range(2):
        at = slice(half * lane, (half + 1) * lane)
        dnormed = total[half * share : (half + 1) * share]
        sums = total[last + 8 * half : last + 8 * half + 8]
        plain = sums[0:1] + sums[2:3]
        cross = sums[1:2] + sums[3:4]
        xhat = xhat_ref[:, at]
        rows_ref[:, at] = (
            (dnormed * gain_ref[...] - plain / width - xhat * (cross / width))
            * inverse_ref[:, at]
        ).astype(BF)
        product = product + dnormed * xhat
    small_ref[0] = heads_ref[...]
    small_ref[0, 7:8, :share] = jnp.sum(product.T, axis=0, keepdims=True)
    small = small_ref[0]
    for at in range(1, small_ref.shape[0]):
        small_ref[at] = small


def finish(width, far, xhat, gain, inverse, head_gains):
    vmem = pl.BlockSpec(memory_space=pltpu.VMEM)
    return pl.pallas_call(
        functools.partial(far_kernel, width),
        in_specs=[vmem] * 5,
        out_specs=[vmem] * 2,
        out_shape=[
            jax.ShapeDtypeStruct(xhat.shape, BF),
            jax.ShapeDtypeStruct((NX * NYL * NC,) + head_gains.shape, F32),
        ],
        compiler_params=pltpu.CompilerParams(vmem_limit_bytes=24 * 2**20),
    )(far, xhat, gain, inverse, head_gains)


def per_device(tokens, layer_norm_gain, w_qkv, q_gain, k_gain, ctx_grad):
    rows, width = tokens.shape
    w_rows, columns = w_qkv.shape
    share = width // (NZ * NYH)
    core = lax.axis_index(DP) % 2
    y_lo = (lax.axis_index(DP) // NC) % NYL
    x_at = lax.axis_index(DP) // (NYL * NC)
    mp = lax.axis_index(MP)
    lane = rows // 2

    with jax.named_scope("gather_w"):
        copies = jnp.broadcast_to(w_qkv[None], (NX * NYL, w_rows, columns))
        own = lax.all_to_all(copies, DP, 0, 0, axis_index_groups=SAME_CORE, tiled=True)
        other = lax.ppermute(own, DP, CORE_SWAP)

    with jax.named_scope("input_norm"):
        x_float = tokens.astype(F32)
        mean = jnp.mean(x_float, axis=-1, keepdims=True)
        centered = x_float - mean
        inverse = lax.rsqrt(jnp.mean(centered * centered, axis=-1, keepdims=True) + 1e-06)
        normed = (centered * inverse * layer_norm_gain).astype(BF)

        extra = jnp.concatenate(
            [jnp.stack(hi_lo(layer_norm_gain)), jnp.zeros((14, width), BF)], axis=0
        )
        lhs = jnp.concatenate([normed, extra], axis=0)

    with jax.named_scope("head"):
        context, dqkv, part, head_gains = run_head(
            core, lhs, own, other, ctx_grad, q_gain, k_gain
        )

    with jax.named_scope("input_gradient_near"):
        near = lax.all_to_all(part, MP, 0, 0, axis_index_groups=NEAR, tiled=True)

    with jax.named_scope("w_grad"):
        term = dot(normed, dqkv, 0, 0).astype(BF).reshape(NX * NYL, NC, w_rows, columns)
        term_keep = jnp.where(core == 0, term[:, 0], term[:, 1])
        term_send = jnp.where(core == 0, term[:, 1], term[:, 0])
        term_got = lax.ppermute(term_send, DP, CORE_SWAP)
        chip = (term_keep.astype(F32) + term_got.astype(F32)).astype(BF)
        chip = chip.reshape(NX, NYL, w_rows, columns)
        x_term = lax.dynamic_index_in_dim(chip, x_at, 0, False).astype(F32)
        leaves = [
            lax.dynamic_index_in_dim(chip, (x_at + step) % NX, 0, False) for step in range(1, NX)
        ]
        x_got = [lax.ppermute(leaf, DP, pairs) for leaf, pairs in zip(leaves, X_STEPS)]

    with jax.named_scope("sum_over_near"):
        start = mp * share
        tokens_share = lax.dynamic_slice_in_dim(tokens, start, share, 1).astype(F32)
        xhat_share = ((tokens_share - mean) * inverse).T
        gain_share = lax.dynamic_slice_in_dim(layer_norm_gain, start, share, 0)[:, None]
        inverse_row = inverse.T
        pair = sum_near(near, leaves + [xhat_share, gain_share, inverse_row])
        far = lax.all_to_all(pair, MP, 0, 0, axis_index_groups=FAR, tiled=True)

    with jax.named_scope("w_grad_y"):
        x_term = x_term + sum(got.astype(F32) for got in x_got)
        leaves = jnp.where(y_lo == 0, x_term[1], x_term[0]).astype(BF)
        stays = jnp.where(y_lo == 0, x_term[0], x_term[1])
        w_grad = (stays + lax.ppermute(leaves, DP, YLO_SWAP).astype(F32)).astype(BF)

    with jax.named_scope("input_gradient"):
        gradient, copies = finish(width, far, xhat_share, gain_share, inverse_row, head_gains)

    with jax.named_scope("gain_gradients"):
        summed = jnp.sum(lax.all_to_all(copies, DP, 0, 0, tiled=True), axis=0)
    return (
        context,
        gradient.T,
        summed[7, :share],
        w_grad,
        summed[0:1],
        summed[1:2],
    )


def solution(mesh):
    placed = (P("dp", None), P(), P("dp", "mp"), P("mp", None), P("mp", None), P("dp", "mp"))
    return jax.shard_map(
        per_device,
        mesh=mesh,
        in_specs=placed,
        out_specs=(
            P("dp", "mp"),
            P("dp", "mp"),
            P("mp"),
            P("dp", "mp"),
            P("mp", None),
            P("mp", None),
        ),
        check_vma=False,
    )
```
